32 devices in a mesh: dp: 4 (over z), pipe: 2 (over core), tensor: 4 (over y, x).
Axes of the slice: x: 2, y: 2, z: 4, core: 2. Of those that a mesh axis runs over, the one named last changes fastest.
Arguments:
- saved_inputs: bfloat16 [2, 4, 128, 1536], P('pipe', 'dp'), may hold values from -40 to 40
- cotangent: bfloat16 [4, 128, 1536], P('dp'), may hold values from -6 to 6
- frame_counts: int32 [4], P('dp'), may hold values from 1 to 128, 320 in all
- glu_weight: bfloat16 [2, 1536, 2, 1536], P('pipe', None, None, 'tensor'), may hold values from -0.15625 to 0.15625
- conv_kernel: float32 [2, 32, 1536], P('pipe', None, 'tensor'), may hold values from -1 to 1
- norm_gain: float32 [2, 1536], P('pipe', 'tensor'), may hold values from 0.5 to 1.5
- norm_bias: float32 [2, 1536], P('pipe', 'tensor'), may hold values from -3 to 3
- out_weight: bfloat16 [2, 1536, 1536], P('pipe', None, 'tensor'), may hold values from -0.15625 to 0.15625
Outputs:
- input_grads: bfloat16 [2, 4, 128, 1536], P('pipe', 'dp', None, 'tensor')
- glu_weight_grad: float32 [2, 1536, 2, 1536], P('pipe', 'dp', None, 'tensor')
- out_weight_grad: float32 [2, 1536, 1536], P('pipe', 'dp', 'tensor')
- kernel_grad: float32 [2, 32, 1536], P('pipe', None, 'tensor')
- gain_grad: float32 [2, 1536], P('pipe', 'tensor')
- bias_grad: float32 [2, 1536], P('pipe', 'tensor')
The draws below stay inside these ranges and needn't reach their ends.
Inputs may be any that keep to these rules, and one draw needn't show every extreme that they name: frame_counts: each utterance has 1 to 128 valid frames and some utterance has exactly 128; slots at or past an utterance's count are padding.
All inputs are finite; a program needn't handle non-finite values. No bound on the sum of `frame_counts` on one device may be relied on, other than what follows from the above.
Results may differ from the reference program's by a relative error of at most 0.01.
Values may be sent and summed in bfloat16 or wider, within the bound.
No kernel may reach another device: no remote copies, remote signals or barrier semaphores. Data moves between devices by JAX's collectives and lax.ppermute only.
A program may use at most 64 MiB of HBM per device.

```python
import math
import jax
import jax.numpy as jnp
import numpy as np
from jax import lax

D = 1536
KERNEL = 32
FRAMES = 128
UTTS = 4
N_TENSOR = 4


def draw_saved_inputs(key, part):
    key_noise, key_rows, key_cols = jax.random.split(jax.random.fold_in(key, 11), 3)
    shape = (2, UTTS, FRAMES, D)
    row_scale = jnp.exp(jax.random.uniform(key_rows, (2, UTTS, FRAMES, 1), jnp.float32, math.log(0.3), math.log(3.0)))
    col_scale = jnp.exp(jax.random.uniform(key_cols, (2, 1, 1, D), jnp.float32, math.log(0.3), math.log(3.0)))
    noise = jnp.clip(jax.random.normal(key_noise, shape, jnp.float32), -4.0, 4.0)
    return (noise * row_scale * col_scale).astype(jnp.bfloat16)


def block_levels(own_key, extent, shards, smallest, high):
    factor_of = 1.0
    for position, shards_of in shards:
        heights = jax.random.uniform(jax.random.fold_in(jax.random.fold_in(own_key, 6), position), (shards_of,), jnp.float32, smallest / len(shards), high / len(shards))
        factor_of = factor_of * jnp.repeat(jnp.exp(heights), extent[position] // shards_of).reshape((-1,) + (1,) * (len(extent) - 1 - position))
    return factor_of


def profile(count, total, most, lean):
    portions = [(1 << 20) // math.isqrt(rank ** lean) + 1 for rank in range(2, count + 1)]
    surplus, counts = total - most - (count - 1), [1] * (count - 1)
    while surplus > 0:
        candidates = [i for i in range(count - 1) if counts[i] < most]
        pool, left = sum([portions[i] for i in candidates]), surplus
        for i in candidates:
            extra = min(most - counts[i], max(1, left * portions[i] // pool), surplus)
            counts[i] = counts[i] + extra
            surplus = surplus - extra
    return np.array([most] + counts)


def ragged_sizes(rng, amount, total, most, slope):
    if amount == 2:
        one = jax.random.randint(rng, (), max(1, total - most), min(most, total - 1) + 1)
        return jnp.stack([one, total - one])
    sizes = jnp.asarray(profile(amount, total, most, slope), jnp.int32)
    twos = (amount - 1) // 2
    source_of, receiver = sizes[1:1 + 2 * twos:2], sizes[2:2 + 2 * twos:2]
    slack = jnp.minimum(source_of - 1, most - receiver)
    passed = jax.random.randint(jax.random.fold_in(rng, 1), (twos,), 0, 1 << 20) % (slack + 1)
    sizes = sizes.at[1:1 + 2 * twos:2].set(source_of - passed).at[2:2 + 2 * twos:2].set(receiver + passed)
    return sizes[jax.random.permutation(jax.random.fold_in(rng, 2), amount)]


def scatter_about(own_key, dims, scale, bound, cuts=(), kind=jnp.bfloat16):
    entries = jax.random.normal(own_key, dims, jnp.float32) * scale
    if len(cuts) > 0:
        entries = block_levels(own_key, dims, cuts, -0.22, 0.18) * entries
    return jnp.clip(entries, min=-bound, max=bound).astype(kind)


def setup_inputs(seed: int = 0) -> dict:
    splits = jax.random.split(jax.random.key(seed), 9)
    return {
        "saved_inputs": draw_saved_inputs(jax.random.fold_in(splits[8], 71), 0),
        "cotangent": scatter_about(splits[1], (UTTS, FRAMES, D), 1.0, 6.0, ((0, 4),)),
        "frame_counts": ragged_sizes(splits[2], UTTS, UTTS * FRAMES * 5 // 8, FRAMES, 2).astype(jnp.int32),
        "glu_weight": scatter_about(splits[3], (2, D, 2, D), D ** -0.5, 0.15625, ((0, 2), (3, 4))),
        "conv_kernel": scatter_about(splits[4], (2, KERNEL, D), KERNEL ** -0.5, 1.0, ((0, 2), (2, 4)), jnp.float32),
        "norm_gain": jnp.clip(0.5 + 1.0 * jax.random.uniform(splits[5], (2, D), jnp.float32) ** block_levels(splits[5], (2, D), ((0, 2), (1, 4)), -0.2, 0.2), 0.5, 1.5),
        "norm_bias": scatter_about(splits[6], (2, D), 0.5, 3.0, ((0, 2), (1, 4)), jnp.float32),
        "out_weight": scatter_about(splits[7], (2, D, D), D ** -0.5, 0.15625, ((0, 2), (2, 4))),
    }


EPSILON = 1e-05

def forward_section(inputs, validity, glu_w, taps, norm_gain, norm_bias):
    left_pad = KERNEL // 2
    projected = jnp.dot(inputs.reshape(-1, D), glu_w.reshape(D, 2 * D), preferred_element_type=jnp.float32).reshape(UTTS, FRAMES, 2, D)
    gated = projected[:, :, 0] * jax.nn.sigmoid(projected[:, :, 1]) * validity
    padded = jnp.pad(gated, ((0, 0), (left_pad, KERNEL - 1 - left_pad), (0, 0)))
    convolved = jnp.zeros_like(gated)
    for tap_index in range(KERNEL):
        convolved = convolved + taps[tap_index] * padded[:, tap_index:tap_index + FRAMES]
    frame_total = jnp.sum(validity)
    center = lax.optimization_barrier(jnp.sum(convolved * validity, axis=(0, 1))) / frame_total
    spread = lax.optimization_barrier(jnp.sum(convolved * convolved * validity, axis=(0, 1))) / frame_total - center * center
    inv_std = lax.rsqrt(spread + EPSILON)
    normed = (convolved - center) * inv_std
    scaled = norm_gain * normed + norm_bias
    squash = jax.nn.sigmoid(scaled)
    activated = (scaled * squash * validity).astype(jnp.bfloat16)
    return (projected, padded, frame_total, inv_std, normed, scaled, squash, activated)

def backward_section(inputs, upstream, validity, glu_w, taps, norm_gain, norm_bias, out_w):
    projected, padded, frame_total, inv_std, normed, scaled, squash, activated = forward_section(inputs, validity, glu_w, taps, norm_gain, norm_bias)
    left_pad = KERNEL // 2
    grad_act = jnp.dot(upstream.reshape(-1, D), out_w, preferred_element_type=jnp.float32).reshape(UTTS, FRAMES, D)
    grad_scaled = grad_act * validity * squash * (1.0 + scaled * (1.0 - squash))
    bias_grad = lax.optimization_barrier(jnp.sum(grad_scaled, axis=(0, 1)))
    gain_grad = lax.optimization_barrier(jnp.sum(grad_scaled * normed, axis=(0, 1)))
    grad_conv = norm_gain * inv_std * (grad_scaled - bias_grad / frame_total - normed * gain_grad / frame_total) * validity
    kernel_grad = jnp.stack([lax.optimization_barrier(jnp.sum(grad_conv * padded[:, tap_index:tap_index + FRAMES], axis=(0, 1))) for tap_index in range(KERNEL)])
    grad_pad = jnp.pad(grad_conv, ((0, 0), (KERNEL - 1 - left_pad, left_pad), (0, 0)))
    grad_gated = jnp.zeros_like(grad_conv)
    for tap_index in range(KERNEL):
        begin = KERNEL - 1 - tap_index
        grad_gated = grad_gated + taps[tap_index] * grad_pad[:, begin:begin + FRAMES]
    grad_gated = grad_gated * validity
    squash_b = jax.nn.sigmoid(projected[:, :, 1])
    grad_proj = jnp.stack([grad_gated * squash_b, grad_gated * projected[:, :, 0] * squash_b * (1.0 - squash_b)], axis=2).astype(jnp.bfloat16)
    inputs_flat = inputs.reshape(-1, D)
    glu_grad = jnp.dot(inputs_flat.T, grad_proj.reshape(-1, 2 * D), preferred_element_type=jnp.float32).reshape(D, 2, D)
    out_grad = jnp.dot(upstream.reshape(-1, D).T, activated.reshape(-1, D), preferred_element_type=jnp.float32)
    channels = D // N_TENSOR
    summed = jnp.zeros((UTTS * FRAMES, D), jnp.float32)
    for group in range(N_TENSOR):
        lower = group * channels
        block_grad = grad_proj[:, :, :, lower:lower + channels].reshape(-1, 2 * channels)
        block_w = glu_w[:, :, lower:lower + channels].reshape(D, 2 * channels)
        partial_value = jnp.dot(block_grad, block_w.T, preferred_element_type=jnp.float32).astype(jnp.bfloat16)
        partial_value = lax.optimization_barrier(partial_value)
        summed = summed + partial_value.astype(jnp.float32)
    input_grad = (upstream.astype(jnp.float32) + summed.reshape(UTTS, FRAMES, D)).astype(jnp.bfloat16)
    return (input_grad, glu_grad, out_grad, kernel_grad, gain_grad, bias_grad)

def reference(saved_inputs, cotangent, frame_counts, glu_weight, conv_kernel, norm_gain, norm_bias, out_weight):
    positions = jnp.arange(FRAMES, dtype=jnp.int32)
    validity = (positions[None, :] < frame_counts[:, None]).astype(jnp.float32)[..., None]
    later = backward_section(saved_inputs[1], cotangent, validity, glu_weight[1], conv_kernel[1], norm_gain[1], norm_bias[1], out_weight[1])
    earlier = backward_section(saved_inputs[0], later[0], validity, glu_weight[0], conv_kernel[0], norm_gain[0], norm_bias[0], out_weight[0])
    return (jnp.stack([earlier[0], later[0]]), jnp.stack([earlier[1], later[1]]), jnp.stack([earlier[2], later[2]]), jnp.stack([earlier[3], later[3]]), jnp.stack([earlier[4], later[4]]), jnp.stack([earlier[5], later[5]]))
```

```python
import functools

import jax
import jax.numpy as jnp
from jax import lax
from jax.experimental import pallas as pl
from jax.experimental.pallas import tpu as pltpu
from jax.sharding import PartitionSpec as P

KERNEL = 32
LEFT = KERNEL // 2
RIGHT = KERNEL - 1 - LEFT
EPSILON = 1e-05
MOST_PERMUTES = 8


def rotated(shard, axis):
    n = lax.axis_size(axis)
    if n > MOST_PERMUTES:
        whole = lax.all_gather(shard, axis)
        return [whole[i] for i in range(n)]
    return [shard] + [
        lax.ppermute(shard, axis, [(i, (i + s) % n) for i in range(n)]) for s in range(1, n)
    ]


def traded(shard, axis, dim):
    n = lax.axis_size(axis)
    block = shard.shape[dim] // n
    if n > MOST_PERMUTES:
        whole = lax.all_to_all(shard, axis, dim, 0, tiled=True)
        size = shard.shape[0]
        return [whole[i * size : (i + 1) * size] for i in range(n)]
    mine = lax.axis_index(axis)
    out = []
    for s in range(n):
        part = lax.dynamic_slice_in_dim(shard, ((mine + s) % n) * block, block, dim)
        out.append(
            part if s == 0 else lax.ppermute(part, axis, [(i, (i + s) % n) for i in range(n)])
        )
    return out


def folded(parts):
    parts = list(parts)
    while len(parts) > 1:
        half = (len(parts) + 1) // 2
        parts = [
            parts[i] + parts[i + half] if i + half < len(parts) else parts[i] for i in range(half)
        ]
    return parts[0]


def summed(shard, axis):
    if lax.axis_size(axis) > MOST_PERMUTES:
        return lax.psum(shard, axis)
    return folded(rotated(shard, axis))


def depthwise(signal, taps, low_pad, high_pad):
    return lax.conv_general_dilated(
        signal,
        taps[:, None, :],
        window_strides=(1,),
        padding=[(low_pad, high_pad)],
        dimension_numbers=("NWC", "WIO", "NWC"),
        feature_group_count=signal.shape[-1],
        precision=lax.Precision.HIGHEST,
    )


def tap_kernel(count, gated_ref, *refs):
    signals, outs, padded = refs[:count], refs[count : 2 * count], refs[2 * count]
    utterances, frames, channels = gated_ref.shape
    padded[...] = jnp.zeros_like(padded)
    for u in range(utterances):
        padded[LEFT : LEFT + frames, :] = gated_ref[u]
        for signal, out in zip(signals, outs):
            for k in range(KERNEL):
                row = jnp.sum(signal[u] * padded[k : k + frames, :], axis=0, keepdims=True)
                if u == 0:
                    out[k : k + 1, :] = row
                else:
                    out[k : k + 1, :] += row


def tap_sums(gated, signals):
    utterances, frames, channels = gated.shape
    count = len(signals)
    work = count * KERNEL * gated.size
    return pl.pallas_call(
        functools.partial(tap_kernel, count),
        out_shape=[jax.ShapeDtypeStruct((KERNEL, channels), jnp.float32)] * count,
        in_specs=[pl.BlockSpec(memory_space=pltpu.VMEM)] * (count + 1),
        out_specs=[pl.BlockSpec(memory_space=pltpu.VMEM)] * count,
        scratch_shapes=[pltpu.VMEM((frames + KERNEL, channels), jnp.float32)],
        cost_estimate=pl.CostEstimate(flops=2 * work, bytes_accessed=4 * work // 8, transcendentals=0),
    )(gated, *signals)


def shards(
    saved_inputs, cotangent, frame_counts, glu_weight, conv_kernel, norm_gain, norm_bias, out_weight
):
    inputs = saved_inputs[0]
    utterances, frames, width = inputs.shape
    channels = out_weight.shape[-1]
    rows = utterances * frames
    tensors = lax.axis_size("tensor")
    tensor_index = lax.axis_index("tensor")
    pipe_index = lax.axis_index("pipe")
    positions = jnp.arange(frames, dtype=jnp.int32)
    validity = (positions[None, :] < frame_counts[:, None]).astype(jnp.float32)[..., None]
    weight = glu_weight[0]
    kernel_taps = conv_kernel[0]
    gain_local = norm_gain[0]
    bias_local = norm_bias[0]
    back_weight = out_weight[0]
    inputs_flat = inputs.reshape(rows, width)

    def product(a, b, dims):
        return lax.dot_general(a, b, (dims, ((), ())), preferred_element_type=jnp.float32)

    projected = product(inputs_flat, weight, ((1,), (0,)))
    linear = projected[:, 0].reshape(utterances, frames, channels)
    gate = jax.nn.sigmoid(projected[:, 1]).reshape(utterances, frames, channels)
    gated = linear * gate * validity
    convolved = depthwise(gated, kernel_taps, LEFT, RIGHT)
    moments = summed(
        jnp.stack(
            [
                jnp.sum(convolved * validity, axis=(0, 1)),
                jnp.sum(convolved * convolved * validity, axis=(0, 1)),
                jnp.broadcast_to(jnp.sum(validity), (channels,)),
            ]
        ),
        "dp",
    )
    frame_total = moments[2]
    center = moments[0] / frame_total
    inv_std = lax.rsqrt(moments[1] / frame_total - center * center + EPSILON)
    normed = (convolved - center) * inv_std
    scaled = gain_local * normed + bias_local
    squash = jax.nn.sigmoid(scaled)
    activated = (scaled * squash * validity).astype(jnp.bfloat16)
    slope = validity * squash * (1.0 + scaled * (1.0 - squash))
    factor = gain_local * inv_std
    ones_taps, normed_taps = tap_sums(
        gated, [jnp.broadcast_to(validity, normed.shape), validity * normed]
    )

    def backward(upstream):
        grad_act = product(upstream.reshape(rows, width), back_weight, ((1,), (0,)))
        grad_scaled = grad_act.reshape(normed.shape) * slope
        sums = summed(
            jnp.stack(
                [jnp.sum(grad_scaled, axis=(0, 1)), jnp.sum(grad_scaled * normed, axis=(0, 1))]
            ),
            "dp",
        )
        bias_grad, gain_grad = sums[0], sums[1]
        grad_conv = (
            factor
            * (grad_scaled - bias_grad / frame_total - normed * (gain_grad / frame_total))
            * validity
        )
        grad_gated = depthwise(grad_conv, kernel_taps[::-1], RIGHT, LEFT) * validity
        grad_proj = jnp.stack(
            [grad_gated * gate, grad_gated * linear * gate * (1.0 - gate)], axis=2
        ).astype(jnp.bfloat16)
        grad_proj = grad_proj.reshape(rows, 2, channels)
        partial = product(grad_proj, weight, ((1, 2), (1, 2))).astype(jnp.bfloat16)
        return partial, grad_proj, grad_scaled, bias_grad, gain_grad

    partial = backward(cotangent)[0]
    arrived = [
        lax.ppermute(
            partial,
            ("pipe", "tensor"),
            [(tensors + i, (i + s) % tensors) for i in range(tensors)],
        ).astype(jnp.float32)
        for s in range(tensors)
    ]
    own = cotangent.astype(jnp.float32)
    first_grad = (own + folded(arrived).reshape(own.shape)).astype(jnp.bfloat16)
    upstream = jnp.where(pipe_index == 1, cotangent, first_grad)

    partial, grad_proj, grad_scaled, bias_grad, gain_grad = backward(upstream)
    reduced = folded([part.astype(jnp.float32) for part in traded(partial, "tensor", 1)])
    upstream_part = lax.dynamic_slice_in_dim(upstream, tensor_index * channels, channels, 2)
    input_grad = (
        upstream_part.astype(jnp.float32) + reduced.reshape(utterances, frames, channels)
    ).astype(jnp.bfloat16)

    (grad_taps,) = tap_sums(gated, [grad_scaled])
    kernel_part = factor * (
        grad_taps
        - (bias_grad / frame_total) * ones_taps
        - (gain_grad / frame_total) * normed_taps
    )
    kernel_grad = summed(kernel_part, "dp")

    all_inputs = jnp.concatenate(traded(inputs_flat, "dp", 1))
    all_upstream = jnp.concatenate(traded(upstream.reshape(rows, width), "dp", 1))
    all_proj = jnp.concatenate(rotated(grad_proj, "dp"))
    all_activated = jnp.concatenate(rotated(activated.reshape(rows, channels), "dp"))
    glu_grad = product(all_inputs, all_proj, ((0,), (0,)))
    out_grad = product(all_upstream, all_activated, ((0,), (0,)))
    return (
        input_grad[None],
        glu_grad[None],
        out_grad[None],
        kernel_grad[None],
        gain_grad[None],
        bias_grad[None],
    )


def solution(mesh):
    placed = (
        P("pipe", "dp", None, None),
        P("dp", None, None),
        P("dp"),
        P("pipe", None, None, "tensor"),
        P("pipe", None, "tensor"),
        P("pipe", "tensor"),
        P("pipe", "tensor"),
        P("pipe", None, "tensor"),
    )
    return jax.shard_map(
        shards,
        mesh=mesh,
        in_specs=placed,
        out_specs=(
            P("pipe", "dp", None, "tensor"),
            P("pipe", "dp", None, "tensor"),
            P("pipe", "dp", "tensor"),
            P("pipe", None, "tensor"),
            P("pipe", "tensor"),
            P("pipe", "tensor"),
        ),
        check_vma=False,
    )
```

```python
import functools

import jax
import jax.numpy as jnp
from jax import lax
from jax.experimental import pallas as pl
from jax.experimental.pallas import tpu as pltpu
from jax.sharding import PartitionSpec as P

KERNEL = 32
LEFT = KERNEL // 2
EPSILON = 1e-05
MOST_PERMUTES = 8
LANES = 128
VMEM_BYTES = 12 << 20
KEPT_ROWS = 8
F32 = jnp.float32
BF16 = jnp.bfloat16
VMEM = pl.BlockSpec(memory_space=pltpu.VMEM)
SMEM = pl.BlockSpec(memory_space=pltpu.SMEM)


def partner(index, n, s):
    return index ^ s if n & (n - 1) == 0 else (index + s) % n


def exchanged(part, axis, s):
    n = lax.axis_size(axis)
    return part if s == 0 else lax.ppermute(part, axis, [(i, partner(i, n, s)) for i in range(n)])


def exchanged_on(part, pipe, s, idle):
    n, tensors = lax.axis_size("dp"), lax.axis_size("tensor")
    pairs = []
    for d in range(n):
        for t in range(tensors):
            here = (2 * d + pipe) * tensors + t
            pairs.append((here, (2 * partner(d, n, s) + pipe) * tensors + t))
            other = (2 * d + 1 - pipe) * tensors
            if idle:
                pairs.append((other + t, other + partner(t, tensors, 1 + s % 2)))
    return lax.ppermute(part, ("dp", "pipe", "tensor"), pairs)


def rotated(shard, axis):
    n = lax.axis_size(axis)
    if n > MOST_PERMUTES:
        whole = lax.all_gather(shard, axis)
        return [whole[i] for i in range(n)]
    return [exchanged(shard, axis, s) for s in range(n)]


def rotated_on(shard, pipe, idle):
    n = lax.axis_size("dp")
    if n > MOST_PERMUTES:
        return rotated(shard, "dp")
    return [shard] + [exchanged_on(shard, pipe, s, idle) for s in range(1, n)]


def traded(shard, axis, dim):
    n = lax.axis_size(axis)
    block = shard.shape[dim] // n
    if n > MOST_PERMUTES:
        whole = lax.all_to_all(shard, axis, dim, 0, tiled=True)
        size = shard.shape[0]
        return [whole[i * size : (i + 1) * size] for i in range(n)]
    mine = lax.axis_index(axis)
    return [
        exchanged(lax.dynamic_slice_in_dim(shard, partner(mine, n, s) * block, block, dim), axis, s)
        for s in range(n)
    ]


def gathered(shard, extra):
    n = lax.axis_size("dp")
    block = shard.shape[1] // n
    mine = lax.axis_index("dp")
    parts = []
    for s in range(n):
        part = lax.dynamic_slice_in_dim(shard, partner(mine, n, s) * block, block, 1)
        parts.append(exchanged(jnp.concatenate([part, extra]), "dp", s))
    return parts


def totals(shard, pipe=None):
    if lax.axis_size("dp") > MOST_PERMUTES:
        return [lax.psum(shard, "dp")]
    return rotated(shard, "dp") if pipe is None else rotated_on(shard, pipe, True)


def tied(first, *others):
    return lax.optimization_barrier((first, *others))


def folded(parts):
    parts = list(parts)
    while len(parts) > 1:
        parts = [
            parts[i] + parts[i + 1] if i + 1 < len(parts) else parts[i]
            for i in range(0, len(parts), 2)
        ]
    return parts[0]


def strips(channels):
    return [slice(low, min(low + LANES, channels)) for low in range(0, channels, LANES)]


def below(rows, block, size):
    return slice(rows.start + block * size, rows.stop + block * size)


def valid_rows(count, frames, lanes):
    rows = lax.broadcasted_iota(jnp.int32, (frames, lanes.stop - lanes.start), 0)
    return (rows < count).astype(F32)


def windows(padded, frames, lanes, offsets):
    for low in range(8):
        mine = [k for k in offsets if k % 8 == low]
        whole = padded[low : max(mine) + frames, lanes]
        for k in mine:
            yield k, whole[k - low : k - low + frames]


def cleared(padded, frames):
    padded[:LEFT, :] = jnp.zeros((LEFT, padded.shape[1]), F32)
    padded[LEFT + frames :, :] = jnp.zeros((padded.shape[0] - LEFT - frames, padded.shape[1]), F32)


def forward_kernel(counts, projected, taps, kept, sums, padded):
    utterances = counts.shape[0]
    size = projected.shape[1]
    frames, channels = size // utterances, projected.shape[2]
    cleared(padded, frames)
    sums[...] = jnp.zeros_like(sums)
    total = sum(counts[u] for u in range(utterances))
    sums[2:3, :] = jnp.full((1, channels), total, jnp.int32).astype(F32)
    kept[4 * size : 4 * size + KERNEL, :] = taps[...]
    for u in range(utterances):
        rows = slice(u * frames, (u + 1) * frames)
        for lanes in strips(channels):
            valid = valid_rows(counts[u], frames, lanes)
            linear = projected[0, rows, lanes]
            gate = jax.nn.sigmoid(projected[1, rows, lanes])
            value = linear * gate * valid
            kept[below(rows, 0, size), lanes] = linear
            kept[below(rows, 1, size), lanes] = gate
            kept[below(rows, 2, size), lanes] = value
            padded[LEFT : LEFT + frames, lanes] = value
            out = jnp.zeros_like(value)
            for k, window in windows(padded, frames, lanes, range(KERNEL)):
                out += taps[k : k + 1, lanes] * window
            kept[below(rows, 3, size), lanes] = out
            part = out * valid
            sums[0:1, lanes] += jnp.sum(part, axis=0, keepdims=True)
            sums[1:2, lanes] += jnp.sum(part * out, axis=0, keepdims=True)


def scaled_sums(sums, u, lanes, grad_scaled, normed):
    rows = [
        jnp.sum(grad_scaled, axis=0, keepdims=True),
        jnp.sum(grad_scaled * normed, axis=0, keepdims=True),
    ]
    for i, row in enumerate(rows):
        if u == 0:
            sums[i : i + 1, lanes] = row
        else:
            sums[i : i + 1, lanes] += row


def norm_kernel(parts, counts, kept, gain, bias, grad_act, *refs):
    moments, (normal, activated, sums) = refs[:parts], refs[parts:]
    utterances = counts.shape[0]
    size, channels = grad_act.shape
    frames = size // utterances
    sums[...] = jnp.zeros_like(sums)
    for lanes in strips(channels):
        moment = folded([part[:, lanes] for part in moments])
        total = moment[2:3]
        center = moment[0:1] / total
        inv_std = lax.rsqrt(moment[1:2] / total - center * center + EPSILON)
        normal[3 * size : 3 * size + 1, lanes] = gain[:, lanes] * inv_std
        normal[3 * size + 1 : 3 * size + 2, lanes] = total
        for u in range(utterances):
            rows = slice(u * frames, (u + 1) * frames)
            valid = valid_rows(counts[u], frames, lanes)
            norm = (kept[below(rows, 3, size), lanes] - center) * inv_std
            scaled = gain[:, lanes] * norm + bias[:, lanes]
            squash = jax.nn.sigmoid(scaled)
            steep = valid * squash * (1.0 + scaled * (1.0 - squash))
            grad = grad_act[rows, lanes] * steep
            normal[below(rows, 0, size), lanes] = norm
            normal[below(rows, 1, size), lanes] = steep
            normal[below(rows, 2, size), lanes] = grad
            activated[rows, lanes] = (scaled * squash * valid).astype(BF16)
            scaled_sums(sums, u, lanes, grad, norm)


def upstream_kernel(parts, later, counts, cotangent, weight, normal, *refs):
    arrived, (upstream, grad_scaled, sums) = refs[:parts], refs[parts:]
    utterances = counts.shape[0]
    size, channels = grad_scaled.shape
    frames = size // utterances
    own = cotangent[...]
    total = own.astype(F32) + folded([part[...].astype(F32) for part in arrived])
    whole = jnp.where(later[0] == 1, own, total.astype(BF16))
    upstream[...] = whole
    grad_act = jnp.dot(whole, weight[...], preferred_element_type=F32)
    sums[...] = jnp.zeros_like(sums)
    for u in range(utterances):
        rows = slice(u * frames, (u + 1) * frames)
        for lanes in strips(channels):
            grad = grad_act[rows, lanes] * normal[below(rows, 1, size), lanes]
            grad_scaled[rows, lanes] = grad
            scaled_sums(sums, u, lanes, grad, normal[below(rows, 0, size), lanes])


def gate_kernel(parts, only_later, later, counts, grad_scaled, kept, normal, tap_table, *refs):
    sums, (grad_taps, *earlier, packed, totals_out, padded) = refs[:parts], refs[parts:]
    utterances = counts.shape[0]
    channels = packed.shape[1]
    size = (packed.shape[0] - KERNEL) // 2
    frames = size // utterances
    base = 2 * size if only_later else 0

    def run():
        cleared(padded, frames)
        total = folded([part[...] for part in sums])
        for ref in earlier:
            total = jnp.where(later[0] == 1, ref[...], total)
        totals_out[...] = total
        for lanes in strips(channels):
            factor = normal[3 * size : 3 * size + 1, lanes]
            frame_total = normal[3 * size + 1 : 3 * size + 2, lanes]
            bias_part = totals_out[0:1, lanes] / frame_total
            gain_part = totals_out[1:2, lanes] / frame_total
            packed[2 * size :, lanes] = (
                factor
                * (
                    grad_taps[:, lanes]
                    - bias_part * tap_table[KERNEL : 2 * KERNEL, lanes]
                    - gain_part * tap_table[:KERNEL, lanes]
                )
            ).astype(BF16)
            for u in range(utterances):
                rows = slice(u * frames, (u + 1) * frames)
                valid = valid_rows(counts[u], frames, lanes)
                grad = grad_scaled[base + rows.start : base + rows.stop, lanes]
                norm = normal[below(rows, 0, size), lanes]
                padded[LEFT : LEFT + frames, lanes] = (
                    factor * (grad - bias_part - norm * gain_part) * valid
                )
                out = jnp.zeros_like(valid)
                for k, window in windows(padded, frames, lanes, range(1, KERNEL + 1)):
                    tap = 4 * size + KERNEL - k
                    out += kept[tap : tap + 1, lanes] * window
                gate = kept[below(rows, 1, size), lanes]
                first = out * valid * gate
                second = first * kept[below(rows, 0, size), lanes] * (1.0 - gate)
                packed[rows, lanes] = first.astype(BF16)
                packed[below(rows, 1, size), lanes] = second.astype(BF16)

    if only_later:
        pl.when(later[0] == 1)(run)
    else:
        run()


def partial_kernel(only_later, later, packed, planes, partial):
    size = partial.shape[0]

    def run():
        out = sum(
            lax.dot_general(
                packed[h * size : (h + 1) * size, :],
                planes[h],
                (((1,), (1,)), ((), ())),
                preferred_element_type=F32,
            )
            for h in range(2)
        )
        partial[...] = out.astype(BF16)

    if only_later:
        pl.when(later[0] == 1)(run)
    else:
        run()


def weights_kernel(parts, *refs):
    ins, (out,) = refs[:-1], refs[-1:]
    pairs = list(zip(ins[:parts], ins[parts:]))
    out[...] = sum(
        lax.dot_general(a[...], b[...], (((0,), (0,)), ((), ())), preferred_element_type=F32)
        for a, b in pairs
    )


def glu_kernel(parts, later, *refs):
    inputs, early, late = (refs[i * parts : (i + 1) * parts] for i in range(3))
    glu_grad, kernel_grad = refs[3 * parts :]
    size = inputs[0].shape[0]
    is_later = later[0] == 1
    for h in range(2):
        rows = slice(h * size, (h + 1) * size)
        glu_grad[:, h, :] = sum(
            lax.dot_general(
                a[...],
                jnp.where(is_later, b[rows, :], c[rows, :]),
                (((0,), (0,)), ((), ())),
                preferred_element_type=F32,
            )
            for a, b, c in zip(inputs, early, late)
        )
    kernel_grad[...] = folded(
        [
            jnp.where(is_later, b[2 * size :, :], c[2 * size :, :]).astype(F32)
            for b, c in zip(early, late)
        ]
    )


def tap_kernel(base, with_ones, counts, kept, signal, out, padded):
    utterances = counts.shape[0]
    frames, channels = padded.shape[0] - KERNEL, out.shape[1]
    size = utterances * frames
    cleared(padded, frames)
    for lanes in strips(channels):
        for u in range(utterances):
            rows = slice(u * frames, (u + 1) * frames)
            valid = valid_rows(counts[u], frames, lanes)
            padded[LEFT : LEFT + frames, lanes] = kept[below(rows, 2, size), lanes]
            factors = [signal[base + rows.start : base + rows.stop, lanes] * valid]
            factors += [valid] if with_ones else []
            for k, window in windows(padded, frames, lanes, range(KERNEL)):
                for i, factor in enumerate(factors):
                    row = jnp.sum(factor * window, axis=0, keepdims=True)
                    at = slice(i * KERNEL + k, i * KERNEL + k + 1)
                    if u == 0:
                        out[at, lanes] = row
                    else:
                        out[at, lanes] += row


def call(kernel, outs, operands, scratch=(), smem=1, flops=0):
    moved = sum(x.size * x.dtype.itemsize for x in operands)
    moved += sum(x.size * x.dtype.itemsize for x in outs)
    return pl.pallas_call(
        kernel,
        out_shape=outs,
        in_specs=[SMEM] * smem + [VMEM] * (len(operands) - smem),
        out_specs=[VMEM] * len(outs),
        scratch_shapes=list(scratch),
        compiler_params=pltpu.CompilerParams(vmem_limit_bytes=VMEM_BYTES),
        cost_estimate=pl.CostEstimate(flops=flops, bytes_accessed=moved, transcendentals=0),
    )(*operands)


def shards(
    saved_inputs, cotangent, frame_counts, glu_weight, conv_kernel, norm_gain, norm_bias, out_weight
):
    inputs = saved_inputs[0]
    utterances, frames, width = inputs.shape
    channels = out_weight.shape[-1]
    rows = utterances * frames
    tensors = lax.axis_size("tensor")
    tensor_index = lax.axis_index("tensor")
    later = lax.axis_index("pipe").astype(jnp.int32).reshape(1)
    weight = glu_weight[0]
    taps = conv_kernel[0]
    back_weight = out_weight[0]
    inputs_flat = inputs.reshape(rows, width)
    cotangent_flat = cotangent.reshape(rows, width)
    shaped = jax.ShapeDtypeStruct
    table = shaped((8, channels), F32)
    taps_shape = shaped((KERNEL, channels), F32)
    padded = pltpu.VMEM((frames + KERNEL, channels), F32)
    conv_work = 2 * KERNEL * rows * channels

    def kept_shape(count, dtype=F32):
        return shaped((max(count, KEPT_ROWS), channels), dtype)

    def product(a, b, dims):
        return lax.dot_general(a, b, (dims, ((), ())), preferred_element_type=F32)

    projected = product(inputs_flat, weight, ((1,), (0,))).transpose(1, 0, 2)
    kept, sums = call(
        forward_kernel,
        [kept_shape(4 * rows + KERNEL), table],
        [frame_counts, projected, taps],
        [padded],
        flops=conv_work,
    )
    sums, weight, cotangent_flat = tied(sums, weight, cotangent_flat)
    planes = weight.transpose(1, 0, 2)
    grad_act = product(cotangent_flat, back_weight, ((1,), (0,)))
    moments = totals(sums)
    normal, activated, sums = call(
        functools.partial(norm_kernel, len(moments)),
        [kept_shape(3 * rows + 8), kept_shape(rows, BF16), table],
        [frame_counts, kept, norm_gain, norm_bias, grad_act, *moments],
    )
    activated = activated[:rows]

    def tap_sums(signal, base, with_ones):
        (out,) = call(
            functools.partial(tap_kernel, base, with_ones),
            [kept_shape(2 * KERNEL) if with_ones else taps_shape],
            [frame_counts, kept, signal],
            [padded],
            flops=conv_work,
        )
        return out

    tap_table = tap_sums(normal, 0, True)
    tap_table, inputs_flat = tied(tap_table, inputs_flat)
    if lax.axis_size("dp") > MOST_PERMUTES:
        all_inputs = traded(inputs_flat, "dp", 1)
        all_activated = rotated(activated, "dp")
    else:
        mixed = gathered(inputs_flat, activated)
        all_inputs, all_activated = [x[:rows] for x in mixed], [x[rows:] for x in mixed]

    def backward(pipe, grad_scaled, sums, earlier):
        parts = totals(sums, pipe)
        grad_taps = tap_sums(grad_scaled, 2 * rows if pipe == 1 else 0, False)
        return call(
            functools.partial(gate_kernel, len(parts), pipe == 1),
            [shaped((2 * rows + KERNEL, channels), BF16), table],
            [later, frame_counts, grad_scaled, kept, normal, tap_table, *parts]
            + [grad_taps, *earlier],
            [padded],
            smem=2,
            flops=conv_work,
        )

    def partial_of(pipe, packed):
        (partial,) = call(
            functools.partial(partial_kernel, pipe == 1),
            [shaped((rows, width), BF16)],
            [later, packed, planes],
            flops=4 * rows * width * channels,
        )
        return partial

    early, total = backward(1, normal, sums, [])
    partial = partial_of(1, early)
    partial, early = tied(partial, early)
    arrived = [
        lax.ppermute(
            partial,
            ("pipe", "tensor"),
            [(tensors + i, (i + s) % tensors) for i in range(tensors)]
            + [(i, tensors + i) for i in range(tensors)],
        )
        for s in range(tensors)
    ]
    all_early = rotated_on(early, 1, False)

    upstream, grad_scaled, sums = call(
        functools.partial(upstream_kernel, len(arrived)),
        [shaped((rows, width), BF16), shaped((rows, channels), F32), table],
        [later, frame_counts, cotangent_flat, back_weight, normal, *arrived],
        smem=2,
        flops=2 * rows * width * channels,
    )
    late, total = backward(0, grad_scaled, sums, [total])
    all_upstream = traded(upstream, "dp", 1)
    all_late = rotated_on(late, 0, True)
    partial = partial_of(0, late)
    reduced = folded([part.astype(F32) for part in traded(partial, "tensor", 1)])
    upstream_part = lax.dynamic_slice_in_dim(upstream, tensor_index * channels, channels, 1)
    input_grad = (upstream_part.astype(F32) + reduced).astype(BF16)

    if len(all_late) > MOST_PERMUTES:
        chosen = jnp.where(later[0] == 1, jnp.stack(all_early), jnp.stack(all_late))
        glu_grad = jnp.einsum(
            "nre,nhrc->ehc",
            jnp.stack(all_inputs),
            chosen[:, : 2 * rows].reshape(-1, 2, rows, channels),
            preferred_element_type=F32,
        )
        kernel_grad = jnp.sum(chosen[:, 2 * rows :].astype(F32), axis=0)
        out_grad = jnp.einsum(
            "nro,nrc->oc",
            jnp.stack(all_upstream),
            jnp.stack(all_activated),
            preferred_element_type=F32,
        )
    else:
        share = width // len(all_late)
        glu_grad, kernel_grad = call(
            functools.partial(glu_kernel, len(all_late)),
            [shaped((share, 2, channels), F32), taps_shape],
            [later, *all_inputs, *all_early, *all_late],
            flops=4 * rows * width * channels,
        )
        (out_grad,) = call(
            functools.partial(weights_kernel, len(all_late)),
            [shaped((share, channels), F32)],
            [*all_upstream, *all_activated],
            smem=0,
            flops=2 * rows * width * channels,
        )
    return (
        input_grad.reshape(1, utterances, frames, channels),
        glu_grad[None],
        out_grad[None],
        kernel_grad[None],
        total[1:2],
        total[0:1],
    )


def solution(mesh):
    placed = (
        P("pipe", "dp", None, None),
        P("dp", None, None),
        P("dp"),
        P("pipe", None, None, "tensor"),
        P("pipe", None, "tensor"),
        P("pipe", "tensor"),
        P("pipe", "tensor"),
        P("pipe", None, "tensor"),
    )
    return jax.shard_map(
        shards,
        mesh=mesh,
        in_specs=placed,
        out_specs=(
            P("pipe", "dp", None, "tensor"),
            P("pipe", "dp", None, "tensor"),
            P("pipe", "dp", "tensor"),
            P("pipe", None, "tensor"),
            P("pipe", "tensor"),
            P("pipe", "tensor"),
        ),
        check_vma=False,
    )
```

```python
import functools

import jax
import jax.numpy as jnp
from jax import lax
from jax.experimental import pallas as pl
from jax.experimental.pallas import tpu as pltpu
from jax.sharding import PartitionSpec as P

D = 1536
KERNEL = 32
LEFT = KERNEL // 2
EPSILON = 1e-05
MOST_PERMUTES = 8
LANES = 128
CODE = 16
VMEM_BYTES = 12 << 20
F32 = jnp.float32
BF16 = jnp.bfloat16
VMEM = pl.BlockSpec(memory_space=pltpu.VMEM)
SMEM = pl.BlockSpec(memory_space=pltpu.SMEM)


def shifted(shard, axis, by):
    devices = lax.axis_size(axis)
    pairs = [(i, i + by) for i in range(devices) if 0 <= i + by < devices]
    return lax.ppermute(shard, axis, pairs)


def depthwise(signal, taps, low_pad, high_pad, channels):
    return lax.conv_general_dilated(
        signal,
        taps[:, None, :],
        window_strides=(1,),
        padding=[(low_pad, high_pad)],
        dimension_numbers=("NWC", "WIO", "NWC"),
        feature_group_count=channels,
        precision=lax.Precision.HIGHEST,
    )


def general_shards(
    saved_inputs, cotangent, frame_counts, glu_weight, conv_kernel, norm_gain, norm_bias, out_weight
):
    channels = D // lax.axis_size("tensor")
    tensor_index = lax.axis_index("tensor")
    pipe_index = lax.axis_index("pipe")
    inputs = saved_inputs[0]
    utterances = inputs.shape[0]
    frames = inputs.shape[1]
    left_pad = KERNEL // 2
    positions = jnp.arange(frames, dtype=jnp.int32)
    validity = (positions[None, :] < frame_counts[:, None]).astype(jnp.float32)[..., None]
    glu_flat = glu_weight[0].reshape(D, 2 * channels)
    kernel_taps = conv_kernel[0]
    gain_local = norm_gain[0]
    bias_local = norm_bias[0]
    back_weight = out_weight[0]
    inputs_flat = inputs.reshape(-1, D)
    projected = jnp.dot(inputs_flat, glu_flat, preferred_element_type=jnp.float32).reshape(
        utterances, frames, 2, channels
    )
    gated = projected[:, :, 0] * jax.nn.sigmoid(projected[:, :, 1]) * validity
    convolved = depthwise(gated, kernel_taps, left_pad, KERNEL - 1 - left_pad, channels)
    moment_sums = lax.psum(
        (
            jnp.sum(convolved * validity, axis=(0, 1)),
            jnp.sum(convolved * convolved * validity, axis=(0, 1)),
            jnp.sum(validity),
        ),
        "dp",
    )
    frame_total = moment_sums[2]
    center = moment_sums[0] / frame_total
    inv_std = lax.rsqrt(moment_sums[1] / frame_total - center * center + EPSILON)
    normed = (convolved - center) * inv_std
    scaled = gain_local * normed + bias_local
    squash = jax.nn.sigmoid(scaled)
    activated = (scaled * squash * validity).astype(jnp.bfloat16)
    padded = jnp.pad(gated, ((0, 0), (left_pad, KERNEL - 1 - left_pad), (0, 0)))
    windows = jnp.stack([padded[:, tap_index : tap_index + frames] for tap_index in range(KERNEL)])
    validity_full = jnp.broadcast_to(validity, normed.shape)
    squash_b = jax.nn.sigmoid(projected[:, :, 1])

    def backward(upstream, with_weights):
        grad_act = jnp.dot(
            upstream.reshape(-1, D), back_weight, preferred_element_type=jnp.float32
        ).reshape(utterances, frames, channels)
        grad_scaled = grad_act * validity * squash * (1.0 + scaled * (1.0 - squash))
        stacked = jnp.stack([grad_scaled, validity_full, validity_full * normed])
        tap_sums = jnp.einsum("jutc,kutc->jkc", stacked, windows, precision=lax.Precision.HIGHEST)
        bias_grad, gain_grad, tap_sums = lax.psum(
            (
                jnp.sum(grad_scaled, axis=(0, 1)),
                jnp.sum(grad_scaled * normed, axis=(0, 1)),
                tap_sums,
            ),
            "dp",
        )
        factor = gain_local * inv_std
        grad_conv = (
            factor
            * (grad_scaled - bias_grad / frame_total - normed * gain_grad / frame_total)
            * validity
        )
        kernel_grad = factor * (
            tap_sums[0]
            - bias_grad / frame_total * tap_sums[1]
            - gain_grad / frame_total * tap_sums[2]
        )
        grad_gated = (
            depthwise(grad_conv, kernel_taps[::-1], KERNEL - 1 - left_pad, left_pad, channels)
            * validity
        )
        grad_proj = jnp.stack(
            [grad_gated * squash_b, grad_gated * projected[:, :, 0] * squash_b * (1.0 - squash_b)],
            axis=2,
        ).astype(jnp.bfloat16)
        grad_flat = grad_proj.reshape(-1, 2 * channels)
        reduced = lax.psum_scatter(
            lax.dot_general(
                glu_flat, grad_flat, (((1,), (1,)), ((), ())), preferred_element_type=jnp.float32
            ).astype(jnp.bfloat16),
            "tensor",
            scatter_dimension=0,
            tiled=True,
        ).astype(jnp.float32)
        upstream_part = lax.dynamic_slice_in_dim(upstream, tensor_index * channels, channels, 2)
        input_grad = (
            upstream_part.astype(jnp.float32) + reduced.T.reshape(utterances, frames, channels)
        ).astype(jnp.bfloat16)
        if not with_weights:
            return (input_grad, None)
        glu_grad = lax.dot_general(
            inputs_flat, grad_flat, (((0,), (0,)), ((), ())), preferred_element_type=jnp.float32
        ).reshape(1, D, 2, channels)
        out_grad = lax.dot_general(
            upstream.reshape(-1, D),
            activated.reshape(-1, channels),
            (((0,), (0,)), ((), ())),
            preferred_element_type=jnp.float32,
        ).reshape(1, D, channels)
        return (input_grad, (glu_grad, out_grad, kernel_grad, gain_grad, bias_grad))

    first_grad = backward(cotangent, False)[0]
    whole = lax.all_gather(first_grad, "tensor", axis=2, tiled=True)
    arrived = shifted(whole, "pipe", -1)
    upstream_now = jnp.where(pipe_index == 1, cotangent, arrived)
    final_grad, weight_parts = backward(upstream_now, True)
    input_grads = final_grad[None]
    glu_grad, out_grad, kernel_grad, gain_grad, bias_grad = weight_parts
    glu_shard, out_shard = (
        lax.psum_scatter(glu_grad, "dp", scatter_dimension=1, tiled=True),
        lax.psum_scatter(out_grad, "dp", scatter_dimension=1, tiled=True),
    )
    return (input_grads, glu_shard, out_shard, kernel_grad[None], gain_grad[None], bias_grad[None])


def swapped(parts, pairs_of):
    sizes = [lax.axis_size(axis) for axis in ("dp", "pipe", "tensor")]
    out = [parts[0]]
    for s in range(1, len(parts)):
        pairs = []
        for d in range(sizes[0]):
            for p in range(sizes[1]):
                for t in range(sizes[2]):
                    e, q, r = pairs_of(s, d, p, t)
                    here = (d * sizes[1] + p) * sizes[2] + t
                    pairs.append((here, (e * sizes[1] + q) * sizes[2] + r))
        out.append(lax.ppermute(parts[s], ("dp", "pipe", "tensor"), pairs))
    return out


def over_dp(s, d, p, t):
    return d ^ s, p, t


def over_tensor(s, d, p, t):
    return d, p, t ^ s


def over_dp_on(pipe):
    return lambda s, d, p, t: over_dp(s, d, p, t) if p == pipe else over_tensor(s, d, p, t)


def tied(first, *others):
    return lax.optimization_barrier((first, *others))


def early_pairs(s, d, p, t):
    return (d ^ s, p, t) if p == 1 else (d ^ 1, p, t)


def folded(parts):
    parts = list(parts)
    while len(parts) > 1:
        parts = [parts[i] + parts[i + 1] for i in range(0, len(parts), 2)]
    return parts[0]


def strips(channels):
    return [slice(low, min(low + LANES, channels)) for low in range(0, channels, LANES)]


def valid_rows(count, frames, lanes):
    rows = lax.broadcasted_iota(jnp.int32, (frames, lanes.stop - lanes.start), 0)
    return (rows < count).astype(F32)


def windows(padded, frames, lanes, offsets):
    for low in range(8):
        mine = [k for k in offsets if k % 8 == low]
        whole = padded[low : max(mine) + frames, lanes]
        for k in mine:
            yield k, whole[k - low : k - low + frames]


def cleared(padded, frames):
    padded[:LEFT, :] = jnp.zeros((LEFT, padded.shape[1]), F32)
    padded[LEFT + frames :, :] = jnp.zeros((padded.shape[0] - LEFT - frames, padded.shape[1]), F32)


def below(rows, block, size):
    return slice(rows.start + block * size, rows.stop + block * size)


def coded(sums, lines):
    value = sums[:lines, :]
    head = value.astype(BF16).astype(F32)
    middle = (value - head).astype(BF16).astype(F32)
    rest = value - head - middle
    blank = jnp.zeros((CODE - 3 * lines, value.shape[1]), F32)
    return jnp.concatenate([head, middle, rest, blank]).astype(BF16)


def decoded(ref, lines, lanes):
    value = ref[:CODE, lanes].astype(F32)
    return value[:lines] + value[lines : 2 * lines] + value[2 * lines : 3 * lines]


def column(index, s, channels):
    return pl.ds(pl.multiple_of((index ^ s) * channels, channels), channels)


def share_rows(place, share):
    return pl.ds(pl.multiple_of(place * share, share), share)


def forward_kernel(place, counts, projected, taps, inputs, kept, payload, padded, sums):
    utterances = counts.shape[0]
    size = projected.shape[1]
    frames, channels = size // utterances, projected.shape[2]
    share = payload.shape[1] - CODE
    cleared(padded, frames)
    sums[...] = jnp.zeros_like(sums)
    total = sum(counts[u] for u in range(utterances))
    sums[2:3, :] = jnp.full((1, channels), total, jnp.int32).astype(F32)
    kept[4 * size : 4 * size + KERNEL, :] = taps[...]
    for u in range(utterances):
        rows = slice(u * frames, (u + 1) * frames)
        for lanes in strips(channels):
            valid = valid_rows(counts[u], frames, lanes)
            linear = projected[0, rows, lanes]
            gate = jax.nn.sigmoid(projected[1, rows, lanes])
            value = linear * gate * valid
            kept[below(rows, 0, size), lanes] = linear
            kept[below(rows, 1, size), lanes] = gate
            kept[below(rows, 2, size), lanes] = value
            padded[LEFT : LEFT + frames, lanes] = value
            out = jnp.zeros_like(value)
            for k, window in windows(padded, frames, lanes, range(KERNEL)):
                out += taps[k : k + 1, lanes] * window
            kept[below(rows, 3, size), lanes] = out
            part = out * valid
            sums[0:1, lanes] += jnp.sum(part, axis=0, keepdims=True)
            sums[1:2, lanes] += jnp.sum(part * out, axis=0, keepdims=True)
    code = coded(sums, 3)
    for s in range(payload.shape[0]):
        payload[s, :CODE, :] = code
        payload[s, CODE:, :] = inputs[share_rows(place[1], share), column(place[0], s, channels)]


def scaled_sums(sums, u, lanes, grad_scaled, normed):
    rows = [
        jnp.sum(grad_scaled, axis=0, keepdims=True),
        jnp.sum(grad_scaled * normed, axis=0, keepdims=True),
    ]
    for i, row in enumerate(rows):
        if u == 0:
            sums[i : i + 1, lanes] = row
        else:
            sums[i : i + 1, lanes] += row


def filled(payload, place, sums, block, source, share):
    channels = payload.shape[2]
    size = block.shape[0]
    code = coded(sums, 2)
    for s in range(payload.shape[0]):
        payload[s, :CODE, :] = code
        payload[s, CODE : CODE + size, :] = block[...]
        payload[s, CODE + size :, :] = source[
            share_rows(place[1], share), column(place[0], s, channels)
        ]


def norm_kernel(place, counts, kept, gain, bias, grad_act, cotangent, *refs):
    *moments, normal, activated, shares, payload, sums = refs
    utterances = counts.shape[0]
    size, channels = grad_act.shape
    frames = size // utterances
    share = size // len(moments)
    sums[...] = jnp.zeros_like(sums)
    for s, part in enumerate(moments):
        shares[s * share : (s + 1) * share, :] = part[CODE:, :]
    for lanes in strips(channels):
        moment = folded([decoded(part, 3, lanes) for part in moments])
        total = moment[2:3]
        center = moment[0:1] / total
        inv_std = lax.rsqrt(moment[1:2] / total - center * center + EPSILON)
        normal[3 * size : 3 * size + 1, lanes] = gain[:, lanes] * inv_std
        normal[3 * size + 1 : 3 * size + 2, lanes] = total
        for u in range(utterances):
            rows = slice(u * frames, (u + 1) * frames)
            valid = valid_rows(counts[u], frames, lanes)
            norm = (kept[below(rows, 3, size), lanes] - center) * inv_std
            scaled = gain[:, lanes] * norm + bias[:, lanes]
            squash = jax.nn.sigmoid(scaled)
            steep = valid * squash * (1.0 + scaled * (1.0 - squash))
            grad = grad_act[rows, lanes] * steep
            normal[below(rows, 0, size), lanes] = norm
            normal[below(rows, 1, size), lanes] = steep
            normal[below(rows, 2, size), lanes] = grad
            activated[rows, lanes] = (scaled * squash * valid).astype(BF16)
            scaled_sums(sums, u, lanes, grad, norm)

    @pl.when(place[2] == 1)
    def _():
        filled(payload, place, sums, activated, cotangent, share)

    @pl.when(place[2] == 0)
    def _():
        filled(payload, place, sums, shares, cotangent, share)


def upstream_kernel(
    parts, place, counts, cotangent, weight, normal, activated, shares, *refs
):
    arrived, (upstream, grad_scaled, payload, sums) = refs[:parts], refs[parts:]
    utterances = counts.shape[0]
    size, channels = grad_scaled.shape
    frames = size // utterances
    share = size // payload.shape[0]
    own = cotangent[...]
    total = own.astype(F32) + folded([part[...].astype(F32) for part in arrived])
    whole = jnp.where(place[2] == 1, own, total.astype(BF16))
    upstream[...] = whole
    grad_act = jnp.dot(whole, weight[...], preferred_element_type=F32)
    sums[...] = jnp.zeros_like(sums)
    for u in range(utterances):
        rows = slice(u * frames, (u + 1) * frames)
        for lanes in strips(channels):
            grad = grad_act[rows, lanes] * normal[below(rows, 1, size), lanes]
            grad_scaled[rows, lanes] = grad
            scaled_sums(sums, u, lanes, grad, normal[below(rows, 0, size), lanes])

    @pl.when(place[2] == 1)
    def _():
        filled(payload, place, sums, shares, upstream, share)

    @pl.when(place[2] == 0)
    def _():
        filled(payload, place, sums, activated, upstream, share)


def gate_kernel(parts, only_later, place, counts, grad_scaled, kept, normal, tap_table, *refs):
    sums, (grad_taps, *earlier, packed, totals_out, padded) = refs[:parts], refs[parts:]
    utterances = counts.shape[0]
    channels = packed.shape[1]
    size = (packed.shape[0] - KERNEL) // 2
    frames = size // utterances
    base = 2 * size if only_later else 0

    def run():
        cleared(padded, frames)
        total = folded([decoded(part, 2, slice(None)) for part in sums])
        for ref in earlier:
            total = jnp.where(place[2] == 1, ref[...], total)
        totals_out[...] = total
        for lanes in strips(channels):
            factor = normal[3 * size : 3 * size + 1, lanes]
            frame_total = normal[3 * size + 1 : 3 * size + 2, lanes]
            bias_part = totals_out[0:1, lanes] / frame_total
            gain_part = totals_out[1:2, lanes] / frame_total
            packed[2 * size :, lanes] = (
                factor
                * (
                    grad_taps[:, lanes]
                    - bias_part * tap_table[KERNEL : 2 * KERNEL, lanes]
                    - gain_part * tap_table[:KERNEL, lanes]
                )
            ).astype(BF16)
            for u in range(utterances):
                rows = slice(u * frames, (u + 1) * frames)
                valid = valid_rows(counts[u], frames, lanes)
                grad = grad_scaled[base + rows.start : base + rows.stop, lanes]
                norm = normal[below(rows, 0, size), lanes]
                padded[LEFT : LEFT + frames, lanes] = (
                    factor * (grad - bias_part - norm * gain_part) * valid
                )
                out = jnp.zeros_like(valid)
                for k, window in windows(padded, frames, lanes, range(1, KERNEL + 1)):
                    tap = 4 * size + KERNEL - k
                    out += kept[tap : tap + 1, lanes] * window
                gate = kept[below(rows, 1, size), lanes]
                first = out * valid * gate
                second = first * kept[below(rows, 0, size), lanes] * (1.0 - gate)
                packed[rows, lanes] = first.astype(BF16)
                packed[below(rows, 1, size), lanes] = second.astype(BF16)

    if only_later:
        pl.when(place[2] == 1)(run)
    else:
        run()


def halves_product(packed, planes, size):
    return sum(
        lax.dot_general(
            packed[h * size : (h + 1) * size, :],
            planes[h],
            (((1,), (1,)), ((), ())),
            preferred_element_type=F32,
        )
        for h in range(2)
    )


def first_partial_kernel(place, packed, planes, partial):
    @pl.when(place[2] == 1)
    def _():
        partial[...] = halves_product(packed, planes, partial.shape[0]).astype(BF16)


def last_partial_kernel(parts, place, packed, planes, *refs):
    early, late, (payload, partial) = refs[:parts], refs[parts : 2 * parts], refs[2 * parts :]
    size = partial.shape[0]
    channels = payload.shape[2]
    share = size // parts
    partial[...] = halves_product(packed, planes, size).astype(BF16)
    for s in range(payload.shape[0]):
        payload[s, :size, :] = partial[:, column(place[1], s, channels)]
        for i in range(parts):
            rows = slice(CODE + size, CODE + size + share)
            value = jnp.where(place[2] == 1, early[i][rows, :], late[i][rows, :])
            payload[s, size + i * share : size + (i + 1) * share, :] = value


def out_kernel(parts, place, upstream, *refs):
    moved, early, late = (refs[i * parts : (i + 1) * parts] for i in range(3))
    input_grad, out_grad, whole = refs[3 * parts :]
    size, channels = input_grad.shape
    share = size // parts
    total = folded([part[:size, :].astype(F32) for part in moved])
    own = upstream[:, column(place[1], 0, channels)]
    input_grad[...] = (own.astype(F32) + total).astype(BF16)
    for j, part in enumerate(moved):
        for i in range(parts):
            rows = slice(size + i * share, size + (i + 1) * share)
            whole[i, share_rows(place[1] ^ j, share), :] = part[rows, :]
    rows = slice(CODE, CODE + size)
    out_grad[...] = sum(
        lax.dot_general(
            whole[i],
            jnp.where(place[2] == 1, early[i][rows, :], late[i][rows, :]),
            (((0,), (0,)), ((), ())),
            preferred_element_type=F32,
        )
        for i in range(parts)
    )


def inputs_kernel(parts, place, *refs):
    early, late, (turned, whole) = refs[:parts], refs[parts : 2 * parts], refs[2 * parts :]
    size = whole.shape[1]
    share = size // parts
    for j in range(parts):
        for i in range(parts):
            rows = slice(CODE + i * share, CODE + (i + 1) * share)
            value = jnp.where(place[2] == 1, late[j][rows, :], early[j][rows, :])
            whole[i, share_rows(place[1] ^ j, share), :] = value
    for i in range(parts):
        turned[:, i * size : (i + 1) * size] = whole[i].astype(F32).T.astype(BF16)


def glu_kernel(parts, place, inputs, *refs):
    early, late, (glu_grad, kernel_grad) = refs[:parts], refs[parts : 2 * parts], refs[2 * parts :]
    size = inputs.shape[1] // parts
    is_later = place[2] == 1
    for h in range(2):
        rows = slice(h * size, (h + 1) * size)
        both = [jnp.where(is_later, b[rows, :], c[rows, :]) for b, c in zip(early, late)]
        glu_grad[:, h, :] = jnp.dot(
            inputs[...], jnp.concatenate(both), preferred_element_type=F32
        )
    kernel_grad[...] = folded(
        [
            jnp.where(is_later, b[2 * size :, :], c[2 * size :, :]).astype(F32)
            for b, c in zip(early, late)
        ]
    )


def tap_kernel(base, with_ones, counts, kept, signal, out, padded):
    utterances = counts.shape[0]
    frames, channels = padded.shape[0] - KERNEL, out.shape[1]
    size = utterances * frames
    cleared(padded, frames)
    for lanes in strips(channels):
        for u in range(utterances):
            rows = slice(u * frames, (u + 1) * frames)
            valid = valid_rows(counts[u], frames, lanes)
            padded[LEFT : LEFT + frames, lanes] = kept[below(rows, 2, size), lanes]
            factors = [signal[base + rows.start : base + rows.stop, lanes] * valid]
            factors += [valid] if with_ones else []
            for k, window in windows(padded, frames, lanes, range(KERNEL)):
                for i, factor in enumerate(factors):
                    row = jnp.sum(factor * window, axis=0, keepdims=True)
                    at = slice(i * KERNEL + k, i * KERNEL + k + 1)
                    if u == 0:
                        out[at, lanes] = row
                    else:
                        out[at, lanes] += row


def call(kernel, outs, operands, scratch=(), smem=0, flops=0, place=None):
    if place is not None:
        inner = kernel
        operands, smem = [*place, *operands], smem + len(place)

        def kernel(d, t, p, *refs):
            inner((d[0], t[0], p[0]), *refs)

    moved = sum(x.size * x.dtype.itemsize for x in operands)
    moved += sum(x.size * x.dtype.itemsize for x in outs)
    return pl.pallas_call(
        kernel,
        out_shape=outs,
        in_specs=[SMEM] * smem + [VMEM] * (len(operands) - smem),
        out_specs=[VMEM] * len(outs),
        scratch_shapes=list(scratch),
        compiler_params=pltpu.CompilerParams(vmem_limit_bytes=VMEM_BYTES),
        cost_estimate=pl.CostEstimate(flops=flops, bytes_accessed=moved, transcendentals=0),
    )(*operands)


def paired_shards(
    saved_inputs, cotangent, frame_counts, glu_weight, conv_kernel, norm_gain, norm_bias, out_weight
):
    inputs = saved_inputs[0]
    utterances, frames, width = inputs.shape
    channels = out_weight.shape[-1]
    rows = utterances * frames
    n = lax.axis_size("dp")
    share = rows // n
    place = [lax.axis_index(axis).astype(jnp.int32).reshape(1) for axis in ("dp", "tensor", "pipe")]
    weight = glu_weight[0]
    taps = conv_kernel[0]
    back_weight = out_weight[0]
    inputs_flat = inputs.reshape(rows, width)
    cotangent_flat = cotangent.reshape(rows, width)
    shaped = jax.ShapeDtypeStruct
    taps_shape = shaped((KERNEL, channels), F32)
    block_shape = shaped((rows, channels), BF16)
    padded = pltpu.VMEM((frames + KERNEL, channels), F32)
    table = pltpu.VMEM((8, channels), F32)
    conv_work = 2 * KERNEL * rows * channels

    def product(a, b, dims):
        return lax.dot_general(a, b, (dims, ((), ())), preferred_element_type=F32)

    projected = product(inputs_flat, weight, ((1,), (0,))).transpose(1, 0, 2)
    kept, payload = call(
        forward_kernel,
        [shaped((4 * rows + KERNEL, channels), F32), shaped((n, CODE + share, channels), BF16)],
        [frame_counts, projected, taps, inputs_flat],
        [padded, table],
        smem=1,
        place=place,
        flops=conv_work,
    )
    grad_act = product(cotangent_flat, back_weight, ((1,), (0,)))
    planes = weight.transpose(1, 0, 2)
    moments = swapped(payload, over_dp)
    normal, activated, shares, payload = call(
        norm_kernel,
        [
            shaped((3 * rows + 8, channels), F32),
            block_shape,
            block_shape,
            shaped((n, CODE + rows + share, channels), BF16),
        ],
        [frame_counts, kept, norm_gain, norm_bias, grad_act, cotangent_flat, *moments],
        [table],
        smem=1,
        place=place,
    )

    def tap_sums(signal, base, with_ones):
        (out,) = call(
            functools.partial(tap_kernel, base, with_ones),
            [shaped((2 * KERNEL, channels), F32) if with_ones else taps_shape],
            [frame_counts, kept, signal],
            [padded],
            smem=1,
            flops=conv_work,
        )
        return out

    tap_table = tap_sums(normal, 0, True)

    def backward(pipe, grad_scaled, payload, earlier, others):
        parts = swapped(payload, over_dp_on(pipe))
        grad_taps = tap_sums(grad_scaled, 2 * rows if pipe == 1 else 0, False)
        grad_taps, *others = tied(grad_taps, *others)
        packed, total = call(
            functools.partial(gate_kernel, n, pipe == 1),
            [shaped((2 * rows + KERNEL, channels), BF16), shaped((2, channels), F32)],
            [frame_counts, grad_scaled, kept, normal, tap_table, *parts]
            + [grad_taps, *earlier],
            [padded],
            smem=1,
        place=place,
            flops=conv_work,
        )
        return packed, total, parts, others

    early, total, early_parts, _ = backward(1, normal, payload, [], [])
    (partial,) = call(
        first_partial_kernel,
        [shaped((rows, width), BF16)],
        [early, planes],
        flops=4 * rows * width * channels,
        place=place,
    )
    arrived = [
        lax.ppermute(
            partial,
            ("pipe", "tensor"),
            [(n + i, (i + s) % n) for i in range(n)] + [(i, n + i) for i in range(n)],
        )
        for s in range(n)
    ]
    all_early = swapped([early] * n, early_pairs)
    upstream, grad_scaled, payload = call(
        functools.partial(upstream_kernel, n),
        [
            shaped((rows, width), BF16),
            shaped((rows, channels), F32),
            shaped((n, CODE + rows + share, channels), BF16),
        ],
        [frame_counts, cotangent_flat, back_weight, normal, activated, shares, *arrived],
        [table],
        smem=1,
        place=place,
        flops=2 * rows * width * channels,
    )
    late, total, late_parts, all_early = backward(0, grad_scaled, payload, [total], all_early)
    all_late = swapped([late] * n, over_dp_on(0))
    (payload,) = call(
        functools.partial(last_partial_kernel, n),
        [shaped((n, 2 * rows, channels), BF16)],
        [late, planes, *early_parts, *late_parts],
        [pltpu.VMEM((rows, width), BF16)],
        flops=4 * rows * width * channels,
        place=place,
    )
    moved = swapped(payload, over_tensor)
    (all_inputs,) = call(
        functools.partial(inputs_kernel, n),
        [shaped((channels, n * rows), BF16)],
        [*early_parts, *late_parts],
        [pltpu.VMEM((n, rows, channels), BF16)],
        place=place,
    )
    glu_grad, kernel_grad = call(
        functools.partial(glu_kernel, n),
        [shaped((channels, 2, channels), F32), taps_shape],
        [all_inputs, *all_early, *all_late],
        flops=4 * rows * width * channels,
        place=place,
    )
    kernel_grad, *moved = tied(kernel_grad, *moved)
    input_grad, out_grad = call(
        functools.partial(out_kernel, n),
        [block_shape, shaped((channels, channels), F32)],
        [upstream, *moved, *early_parts, *late_parts],
        [pltpu.VMEM((n, rows, channels), BF16)],
        flops=2 * rows * width * channels,
        place=place,
    )
    return (
        input_grad.reshape(1, utterances, frames, channels),
        glu_grad[None],
        out_grad[None],
        kernel_grad[None],
        total[1:2],
        total[0:1],
    )


def solution(mesh):
    placed = (
        P("pipe", "dp", None, None),
        P("dp", None, None),
        P("dp"),
        P("pipe", None, None, "tensor"),
        P("pipe", None, "tensor"),
        P("pipe", "tensor"),
        P("pipe", "tensor"),
        P("pipe", None, "tensor"),
    )
    n = mesh.shape["dp"]
    paired = n == mesh.shape["tensor"] and n in (2, 4, 8) and mesh.shape["pipe"] == 2
    return jax.shard_map(
        paired_shards if paired else general_shards,
        mesh=mesh,
        in_specs=placed,
        out_specs=(
            P("pipe", "dp", None, "tensor"),
            P("pipe", "dp", None, "tensor"),
            P("pipe", "dp", "tensor"),
            P("pipe", None, "tensor"),
            P("pipe", "tensor"),
            P("pipe", "tensor"),
        ),
        check_vma=False,
    )
```

```python
import functools

import jax
import jax.numpy as jnp
from jax import lax
from jax.experimental import pallas as pl
from jax.experimental.pallas import tpu as pltpu
from jax.sharding import PartitionSpec as P

D = 1536
KERNEL = 32
LEFT = KERNEL // 2
EPSILON = 1e-05
MOST_PERMUTES = 8
LANES = 128
CODE = 16
VMEM_BYTES = 12 << 20
F32 = jnp.float32
BF16 = jnp.bfloat16
VMEM = pl.BlockSpec(memory_space=pltpu.VMEM)
SMEM = pl.BlockSpec(memory_space=pltpu.SMEM)


def shifted(shard, axis, by):
    devices = lax.axis_size(axis)
    pairs = [(i, i + by) for i in range(devices) if 0 <= i + by < devices]
    return lax.ppermute(shard, axis, pairs)


def depthwise(signal, taps, low_pad, high_pad, channels):
    return lax.conv_general_dilated(
        signal,
        taps[:, None, :],
        window_strides=(1,),
        padding=[(low_pad, high_pad)],
        dimension_numbers=("NWC", "WIO", "NWC"),
        feature_group_count=channels,
        precision=lax.Precision.HIGHEST,
    )


def general_shards(
    saved_inputs, cotangent, frame_counts, glu_weight, conv_kernel, norm_gain, norm_bias, out_weight
):
    channels = D // lax.axis_size("tensor")
    tensor_index = lax.axis_index("tensor")
    pipe_index = lax.axis_index("pipe")
    inputs = saved_inputs[0]
    utterances = inputs.shape[0]
    frames = inputs.shape[1]
    left_pad = KERNEL // 2
    positions = jnp.arange(frames, dtype=jnp.int32)
    validity = (positions[None, :] < frame_counts[:, None]).astype(jnp.float32)[..., None]
    glu_flat = glu_weight[0].reshape(D, 2 * channels)
    kernel_taps = conv_kernel[0]
    gain_local = norm_gain[0]
    bias_local = norm_bias[0]
    back_weight = out_weight[0]
    inputs_flat = inputs.reshape(-1, D)
    projected = jnp.dot(inputs_flat, glu_flat, preferred_element_type=jnp.float32).reshape(
        utterances, frames, 2, channels
    )
    gated = projected[:, :, 0] * jax.nn.sigmoid(projected[:, :, 1]) * validity
    convolved = depthwise(gated, kernel_taps, left_pad, KERNEL - 1 - left_pad, channels)
    moment_sums = lax.psum(
        (
            jnp.sum(convolved * validity, axis=(0, 1)),
            jnp.sum(convolved * convolved * validity, axis=(0, 1)),
            jnp.sum(validity),
        ),
        "dp",
    )
    frame_total = moment_sums[2]
    center = moment_sums[0] / frame_total
    inv_std = lax.rsqrt(moment_sums[1] / frame_total - center * center + EPSILON)
    normed = (convolved - center) * inv_std
    scaled = gain_local * normed + bias_local
    squash = jax.nn.sigmoid(scaled)
    activated = (scaled * squash * validity).astype(jnp.bfloat16)
    padded = jnp.pad(gated, ((0, 0), (left_pad, KERNEL - 1 - left_pad), (0, 0)))
    windows = jnp.stack([padded[:, tap_index : tap_index + frames] for tap_index in range(KERNEL)])
    validity_full = jnp.broadcast_to(validity, normed.shape)
    squash_b = jax.nn.sigmoid(projected[:, :, 1])

    def backward(upstream, with_weights):
        grad_act = jnp.dot(
            upstream.reshape(-1, D), back_weight, preferred_element_type=jnp.float32
        ).reshape(utterances, frames, channels)
        grad_scaled = grad_act * validity * squash * (1.0 + scaled * (1.0 - squash))
        stacked = jnp.stack([grad_scaled, validity_full, validity_full * normed])
        tap_sums = jnp.einsum("jutc,kutc->jkc", stacked, windows, precision=lax.Precision.HIGHEST)
        bias_grad, gain_grad, tap_sums = lax.psum(
            (
                jnp.sum(grad_scaled, axis=(0, 1)),
                jnp.sum(grad_scaled * normed, axis=(0, 1)),
                tap_sums,
            ),
            "dp",
        )
        factor = gain_local * inv_std
        grad_conv = (
            factor
            * (grad_scaled - bias_grad / frame_total - normed * gain_grad / frame_total)
            * validity
        )
        kernel_grad = factor * (
            tap_sums[0]
            - bias_grad / frame_total * tap_sums[1]
            - gain_grad / frame_total * tap_sums[2]
        )
        grad_gated = (
            depthwise(grad_conv, kernel_taps[::-1], KERNEL - 1 - left_pad, left_pad, channels)
            * validity
        )
        grad_proj = jnp.stack(
            [grad_gated * squash_b, grad_gated * projected[:, :, 0] * squash_b * (1.0 - squash_b)],
            axis=2,
        ).astype(jnp.bfloat16)
        grad_flat = grad_proj.reshape(-1, 2 * channels)
        reduced = lax.psum_scatter(
            lax.dot_general(
                glu_flat, grad_flat, (((1,), (1,)), ((), ())), preferred_element_type=jnp.float32
            ).astype(jnp.bfloat16),
            "tensor",
            scatter_dimension=0,
            tiled=True,
        ).astype(jnp.float32)
        upstream_part = lax.dynamic_slice_in_dim(upstream, tensor_index * channels, channels, 2)
        input_grad = (
            upstream_part.astype(jnp.float32) + reduced.T.reshape(utterances, frames, channels)
        ).astype(jnp.bfloat16)
        if not with_weights:
            return (input_grad, None)
        glu_grad = lax.dot_general(
            inputs_flat, grad_flat, (((0,), (0,)), ((), ())), preferred_element_type=jnp.float32
        ).reshape(1, D, 2, channels)
        out_grad = lax.dot_general(
            upstream.reshape(-1, D),
            activated.reshape(-1, channels),
            (((0,), (0,)), ((), ())),
            preferred_element_type=jnp.float32,
        ).reshape(1, D, channels)
        return (input_grad, (glu_grad, out_grad, kernel_grad, gain_grad, bias_grad))

    first_grad = backward(cotangent, False)[0]
    whole = lax.all_gather(first_grad, "tensor", axis=2, tiled=True)
    arrived = shifted(whole, "pipe", -1)
    upstream_now = jnp.where(pipe_index == 1, cotangent, arrived)
    final_grad, weight_parts = backward(upstream_now, True)
    input_grads = final_grad[None]
    glu_grad, out_grad, kernel_grad, gain_grad, bias_grad = weight_parts
    glu_shard, out_shard = (
        lax.psum_scatter(glu_grad, "dp", scatter_dimension=1, tiled=True),
        lax.psum_scatter(out_grad, "dp", scatter_dimension=1, tiled=True),
    )
    return (input_grads, glu_shard, out_shard, kernel_grad[None], gain_grad[None], bias_grad[None])


def swapped(parts, pairs_of):
    sizes = [lax.axis_size(axis) for axis in ("dp", "pipe", "tensor")]
    out = [parts[0]]
    for s in range(1, len(parts)):
        pairs = []
        for d in range(sizes[0]):
            for p in range(sizes[1]):
                for t in range(sizes[2]):
                    e, q, r = pairs_of(s, d, p, t)
                    here = (d * sizes[1] + p) * sizes[2] + t
                    pairs.append((here, (e * sizes[1] + q) * sizes[2] + r))
        out.append(lax.ppermute(parts[s], ("dp", "pipe", "tensor"), pairs))
    return out


def over_dp(s, d, p, t):
    return d ^ s, p, t


def over_tensor(s, d, p, t):
    return d, p, t ^ s


def over_dp_on(pipe):
    return lambda s, d, p, t: over_dp(s, d, p, t) if p == pipe else over_tensor(s, d, p, t)


def tied(first, *others):
    return lax.optimization_barrier((first, *others))


def early_pairs(s, d, p, t):
    return (d ^ s, p, t) if p == 1 else (d ^ 1, p, t)


def folded(parts):
    parts = list(parts)
    while len(parts) > 1:
        parts = [parts[i] + parts[i + 1] for i in range(0, len(parts), 2)]
    return parts[0]


def strips(channels):
    return [slice(low, min(low + LANES, channels)) for low in range(0, channels, LANES)]


def valid_rows(count, frames, lanes):
    rows = lax.broadcasted_iota(jnp.int32, (frames, lanes.stop - lanes.start), 0)
    return (rows < count).astype(F32)


def windows(padded, frames, lanes, offsets):
    for low in range(8):
        mine = [k for k in offsets if k % 8 == low]
        whole = padded[low : max(mine) + frames, lanes]
        for k in mine:
            yield k, whole[k - low : k - low + frames]


def cleared(padded, frames):
    padded[:LEFT, :] = jnp.zeros((LEFT, padded.shape[1]), F32)
    padded[LEFT + frames :, :] = jnp.zeros((padded.shape[0] - LEFT - frames, padded.shape[1]), F32)


def below(rows, block, size):
    return slice(rows.start + block * size, rows.stop + block * size)


def coded(sums, lines):
    value = sums[:lines, :]
    head = value.astype(BF16).astype(F32)
    middle = (value - head).astype(BF16).astype(F32)
    rest = value - head - middle
    blank = jnp.zeros((CODE - 3 * lines, value.shape[1]), F32)
    return jnp.concatenate([head, middle, rest, blank]).astype(BF16)


def decoded(ref, lines, lanes):
    value = ref[:CODE, lanes].astype(F32)
    return value[:lines] + value[lines : 2 * lines] + value[2 * lines : 3 * lines]


def column(index, s, channels):
    return pl.ds(pl.multiple_of((index ^ s) * channels, channels), channels)


def share_rows(place, share):
    return pl.ds(pl.multiple_of(place * share, share), share)


def forward_kernel(place, counts, projected, taps, inputs, kept, payload, padded, sums):
    utterances = counts.shape[0]
    size = projected.shape[1]
    frames, channels = size // utterances, projected.shape[2]
    share = payload.shape[1] - CODE
    cleared(padded, frames)
    sums[...] = jnp.zeros_like(sums)
    total = sum(counts[u] for u in range(utterances))
    sums[2:3, :] = jnp.full((1, channels), total, jnp.int32).astype(F32)
    kept[4 * size : 4 * size + KERNEL, :] = taps[...]
    for u in range(utterances):
        rows = slice(u * frames, (u + 1) * frames)
        for lanes in strips(channels):
            valid = valid_rows(counts[u], frames, lanes)
            linear = projected[0, rows, lanes]
            gate = jax.nn.sigmoid(projected[1, rows, lanes])
            value = linear * gate * valid
            kept[below(rows, 0, size), lanes] = linear
            kept[below(rows, 1, size), lanes] = gate
            kept[below(rows, 2, size), lanes] = value
            padded[LEFT : LEFT + frames, lanes] = value
            out = jnp.zeros_like(value)
            for k, window in windows(padded, frames, lanes, range(KERNEL)):
                out += taps[k : k + 1, lanes] * window
            kept[below(rows, 3, size), lanes] = out
            part = out * valid
            sums[0:1, lanes] += jnp.sum(part, axis=0, keepdims=True)
            sums[1:2, lanes] += jnp.sum(part * out, axis=0, keepdims=True)
    code = coded(sums, 3)
    for s in range(payload.shape[0]):
        payload[s, :CODE, :] = code
        payload[s, CODE:, :] = inputs[share_rows(place[1], share), column(place[0], s, channels)]


def scaled_sums(sums, u, lanes, grad_scaled, normed):
    rows = [
        jnp.sum(grad_scaled, axis=0, keepdims=True),
        jnp.sum(grad_scaled * normed, axis=0, keepdims=True),
    ]
    for i, row in enumerate(rows):
        if u == 0:
            sums[i : i + 1, lanes] = row
        else:
            sums[i : i + 1, lanes] += row


def filled(payload, place, sums, block, source, share):
    channels = payload.shape[2]
    size = block.shape[0]
    code = coded(sums, 2)
    for s in range(payload.shape[0]):
        payload[s, :CODE, :] = code
        payload[s, CODE : CODE + size, :] = block[...]
        payload[s, CODE + size :, :] = source[
            share_rows(place[1], share), column(place[0], s, channels)
        ]


def norm_kernel(place, counts, kept, gain, bias, grad_act, cotangent, *refs):
    *moments, normal, activated, shares, payload, sums = refs
    moments = moments[::-1]
    utterances = counts.shape[0]
    size, channels = grad_act.shape
    frames = size // utterances
    share = size // len(moments)
    sums[...] = jnp.zeros_like(sums)
    for s, part in enumerate(moments):
        shares[s * share : (s + 1) * share, :] = part[CODE:, :]
    for lanes in strips(channels):
        moment = folded([decoded(part, 3, lanes) for part in moments])
        total = moment[2:3]
        center = moment[0:1] / total
        inv_std = lax.rsqrt(moment[1:2] / total - center * center + EPSILON)
        normal[3 * size : 3 * size + 1, lanes] = gain[:, lanes] * inv_std
        normal[3 * size + 1 : 3 * size + 2, lanes] = total
        for u in range(utterances):
            rows = slice(u * frames, (u + 1) * frames)
            valid = valid_rows(counts[u], frames, lanes)
            norm = (kept[below(rows, 3, size), lanes] - center) * inv_std
            scaled = gain[:, lanes] * norm + bias[:, lanes]
            squash = jax.nn.sigmoid(scaled)
            steep = valid * squash * (1.0 + scaled * (1.0 - squash))
            grad = grad_act[rows, lanes] * steep
            normal[below(rows, 0, size), lanes] = norm
            normal[below(rows, 1, size), lanes] = steep
            normal[below(rows, 2, size), lanes] = grad
            activated[rows, lanes] = (scaled * squash * valid).astype(BF16)
            scaled_sums(sums, u, lanes, grad, norm)

    @pl.when(place[2] == 1)
    def _():
        filled(payload, place, sums, activated, cotangent, share)

    @pl.when(place[2] == 0)
    def _():
        filled(payload, place, sums, shares, cotangent, share)


def upstream_kernel(
    parts, place, counts, cotangent, weight, normal, activated, shares, *refs
):
    arrived, (upstream, grad_scaled, payload, sums) = refs[:parts], refs[parts:]
    utterances = counts.shape[0]
    size, channels = grad_scaled.shape
    frames = size // utterances
    share = size // payload.shape[0]
    own = cotangent[...]
    total = own.astype(F32) + folded([part[...].astype(F32) for part in arrived])
    whole = jnp.where(place[2] == 1, own, total.astype(BF16))
    upstream[...] = whole
    grad_act = jnp.dot(whole, weight[...], preferred_element_type=F32)
    sums[...] = jnp.zeros_like(sums)
    for u in range(utterances):
        rows = slice(u * frames, (u + 1) * frames)
        for lanes in strips(channels):
            grad = grad_act[rows, lanes] * normal[below(rows, 1, size), lanes]
            grad_scaled[rows, lanes] = grad
            scaled_sums(sums, u, lanes, grad, normal[below(rows, 0, size), lanes])

    @pl.when(place[2] == 1)
    def _():
        filled(payload, place, sums, shares, upstream, share)

    @pl.when(place[2] == 0)
    def _():
        filled(payload, place, sums, activated, upstream, share)


def gate_kernel(parts, only_later, place, counts, grad_scaled, kept, normal, tap_table, *refs):
    sums, (grad_taps, *earlier, packed, totals_out, padded) = refs[:parts][::-1], refs[parts:]
    utterances = counts.shape[0]
    channels = packed.shape[1]
    size = (packed.shape[0] - KERNEL) // 2
    frames = size // utterances
    base = 2 * size if only_later else 0

    def run():
        cleared(padded, frames)
        total = folded([decoded(part, 2, slice(None)) for part in sums])
        for ref in earlier:
            total = jnp.where(place[2] == 1, ref[...], total)
        totals_out[...] = total
        for lanes in strips(channels):
            factor = normal[3 * size : 3 * size + 1, lanes]
            frame_total = normal[3 * size + 1 : 3 * size + 2, lanes]
            bias_part = totals_out[0:1, lanes] / frame_total
            gain_part = totals_out[1:2, lanes] / frame_total
            packed[2 * size :, lanes] = (
                factor
                * (
                    grad_taps[:, lanes]
                    - bias_part * tap_table[KERNEL : 2 * KERNEL, lanes]
                    - gain_part * tap_table[:KERNEL, lanes]
                )
            ).astype(BF16)
            for u in range(utterances):
                rows = slice(u * frames, (u + 1) * frames)
                valid = valid_rows(counts[u], frames, lanes)
                grad = grad_scaled[base + rows.start : base + rows.stop, lanes]
                norm = normal[below(rows, 0, size), lanes]
                padded[LEFT : LEFT + frames, lanes] = (
                    factor * (grad - bias_part - norm * gain_part) * valid
                )
                out = jnp.zeros_like(valid)
                for k, window in windows(padded, frames, lanes, range(1, KERNEL + 1)):
                    tap = 4 * size + KERNEL - k
                    out += kept[tap : tap + 1, lanes] * window
                gate = kept[below(rows, 1, size), lanes]
                first = out * valid * gate
                second = first * kept[below(rows, 0, size), lanes] * (1.0 - gate)
                packed[rows, lanes] = first.astype(BF16)
                packed[below(rows, 1, size), lanes] = second.astype(BF16)

    if only_later:
        pl.when(place[2] == 1)(run)
    else:
        run()


def halves_product(packed, planes, size):
    return sum(
        lax.dot_general(
            packed[h * size : (h + 1) * size, :],
            planes[h],
            (((1,), (1,)), ((), ())),
            preferred_element_type=F32,
        )
        for h in range(2)
    )


def first_partial_kernel(place, packed, planes, partial):
    @pl.when(place[2] == 1)
    def _():
        partial[...] = halves_product(packed, planes, partial.shape[0]).astype(BF16)


def last_partial_kernel(parts, place, packed, planes, *refs):
    early, late, (payload, partial) = refs[:parts], refs[parts : 2 * parts], refs[2 * parts :]
    size = partial.shape[0]
    channels = payload.shape[2]
    share = size // parts
    partial[...] = halves_product(packed, planes, size).astype(BF16)
    for s in range(payload.shape[0]):
        payload[s, :size, :] = partial[:, column(place[1], s, channels)]
        for i in range(parts):
            rows = slice(CODE + size, CODE + size + share)
            value = jnp.where(place[2] == 1, early[i][rows, :], late[i][rows, :])
            payload[s, size + i * share : size + (i + 1) * share, :] = value


def out_kernel(parts, place, upstream, *refs):
    moved, early, late = (refs[i * parts : (i + 1) * parts] for i in range(3))
    moved = moved[::-1]
    input_grad, out_grad, whole = refs[3 * parts :]
    size, channels = input_grad.shape
    share = size // parts
    total = folded([part[:size, :].astype(F32) for part in moved])
    own = upstream[:, column(place[1], 0, channels)]
    input_grad[...] = (own.astype(F32) + total).astype(BF16)
    for j, part in enumerate(moved):
        for i in range(parts):
            rows = slice(size + i * share, size + (i + 1) * share)
            whole[i, share_rows(place[1] ^ j, share), :] = part[rows, :]
    rows = slice(CODE, CODE + size)
    out_grad[...] = sum(
        lax.dot_general(
            whole[i],
            jnp.where(place[2] == 1, early[i][rows, :], late[i][rows, :]),
            (((0,), (0,)), ((), ())),
            preferred_element_type=F32,
        )
        for i in range(parts)
    )


def inputs_kernel(parts, place, *refs):
    early, late, (turned, whole) = refs[:parts], refs[parts : 2 * parts], refs[2 * parts :]
    size = whole.shape[1]
    share = size // parts
    for j in range(parts):
        for i in range(parts):
            rows = slice(CODE + i * share, CODE + (i + 1) * share)
            value = jnp.where(place[2] == 1, late[j][rows, :], early[j][rows, :])
            whole[i, share_rows(place[1] ^ j, share), :] = value
    for i in range(parts):
        turned[:, i * size : (i + 1) * size] = whole[i].astype(F32).T.astype(BF16)


def glu_kernel(parts, place, inputs, *refs):
    early, late, (glu_grad, kernel_grad) = refs[:parts], refs[parts : 2 * parts], refs[2 * parts :]
    early, late = early[::-1], late[::-1]
    size = inputs.shape[1] // parts
    is_later = place[2] == 1
    for h in range(2):
        rows = slice(h * size, (h + 1) * size)
        both = [jnp.where(is_later, b[rows, :], c[rows, :]) for b, c in zip(early, late)]
        glu_grad[:, h, :] = jnp.dot(
            inputs[...], jnp.concatenate(both), preferred_element_type=F32
        )
    kernel_grad[...] = folded(
        [
            jnp.where(is_later, b[2 * size :, :], c[2 * size :, :]).astype(F32)
            for b, c in zip(early, late)
        ]
    )


def tap_kernel(base, with_ones, counts, kept, signal, out, padded):
    utterances = counts.shape[0]
    frames, channels = padded.shape[0] - KERNEL, out.shape[1]
    size = utterances * frames
    cleared(padded, frames)
    for lanes in strips(channels):
        for u in range(utterances):
            rows = slice(u * frames, (u + 1) * frames)
            valid = valid_rows(counts[u], frames, lanes)
            padded[LEFT : LEFT + frames, lanes] = kept[below(rows, 2, size), lanes]
            factors = [signal[base + rows.start : base + rows.stop, lanes] * valid]
            factors += [valid] if with_ones else []
            for k, window in windows(padded, frames, lanes, range(KERNEL)):
                for i, factor in enumerate(factors):
                    row = jnp.sum(factor * window, axis=0, keepdims=True)
                    at = slice(i * KERNEL + k, i * KERNEL + k + 1)
                    if u == 0:
                        out[at, lanes] = row
                    else:
                        out[at, lanes] += row


def call(kernel, outs, operands, scratch=(), smem=0, flops=0, place=None):
    if place is not None:
        inner = kernel
        operands, smem = [*place, *operands], smem + len(place)

        def kernel(d, t, p, *refs):
            inner((d[0], t[0], p[0]), *refs)

    moved = sum(x.size * x.dtype.itemsize for x in operands)
    moved += sum(x.size * x.dtype.itemsize for x in outs)
    return pl.pallas_call(
        kernel,
        out_shape=outs,
        in_specs=[SMEM] * smem + [VMEM] * (len(operands) - smem),
        out_specs=[VMEM] * len(outs),
        scratch_shapes=list(scratch),
        compiler_params=pltpu.CompilerParams(vmem_limit_bytes=VMEM_BYTES),
        cost_estimate=pl.CostEstimate(flops=flops, bytes_accessed=moved, transcendentals=0),
    )(*operands)


def paired_shards(
    saved_inputs, cotangent, frame_counts, glu_weight, conv_kernel, norm_gain, norm_bias, out_weight
):
    inputs = saved_inputs[0]
    utterances, frames, width = inputs.shape
    channels = out_weight.shape[-1]
    rows = utterances * frames
    n = lax.axis_size("dp")
    share = rows // n
    place = [lax.axis_index(axis).astype(jnp.int32).reshape(1) for axis in ("dp", "tensor", "pipe")]
    weight = glu_weight[0]
    taps = conv_kernel[0]
    back_weight = out_weight[0]
    inputs_flat = inputs.reshape(rows, width)
    cotangent_flat = cotangent.reshape(rows, width)
    shaped = jax.ShapeDtypeStruct
    taps_shape = shaped((KERNEL, channels), F32)
    block_shape = shaped((rows, channels), BF16)
    padded = pltpu.VMEM((frames + KERNEL, channels), F32)
    table = pltpu.VMEM((8, channels), F32)
    conv_work = 2 * KERNEL * rows * channels

    def product(a, b, dims):
        return lax.dot_general(a, b, (dims, ((), ())), preferred_element_type=F32)

    projected = product(inputs_flat, weight, ((1,), (0,))).transpose(1, 0, 2)
    kept, payload = call(
        forward_kernel,
        [shaped((4 * rows + KERNEL, channels), F32), shaped((n, CODE + share, channels), BF16)],
        [frame_counts, projected, taps, inputs_flat],
        [padded, table],
        smem=1,
        place=place,
        flops=conv_work,
    )
    grad_act = product(cotangent_flat, back_weight, ((1,), (0,)))
    planes = weight.transpose(1, 0, 2)
    moments = swapped(payload, over_dp)
    normal, activated, shares, payload = call(
        norm_kernel,
        [
            shaped((3 * rows + 8, channels), F32),
            block_shape,
            block_shape,
            shaped((n, CODE + rows + share, channels), BF16),
        ],
        [frame_counts, kept, norm_gain, norm_bias, grad_act, cotangent_flat, *moments[::-1]],
        [table],
        smem=1,
        place=place,
    )

    def tap_sums(signal, base, with_ones):
        (out,) = call(
            functools.partial(tap_kernel, base, with_ones),
            [shaped((2 * KERNEL, channels), F32) if with_ones else taps_shape],
            [frame_counts, kept, signal],
            [padded],
            smem=1,
            flops=conv_work,
        )
        return out

    tap_table = tap_sums(normal, 0, True)

    def backward(pipe, grad_scaled, payload, earlier, others):
        parts = swapped(payload, over_dp_on(pipe))
        grad_taps = tap_sums(grad_scaled, 2 * rows if pipe == 1 else 0, False)
        grad_taps, *others = tied(grad_taps, *others)
        packed, total = call(
            functools.partial(gate_kernel, n, pipe == 1),
            [shaped((2 * rows + KERNEL, channels), BF16), shaped((2, channels), F32)],
            [frame_counts, grad_scaled, kept, normal, tap_table, *parts[::-1]]
            + [grad_taps, *earlier],
            [padded],
            smem=1,
        place=place,
            flops=conv_work,
        )
        return packed, total, parts, others

    early, total, early_parts, _ = backward(1, normal, payload, [], [])
    (partial,) = call(
        first_partial_kernel,
        [shaped((rows, width), BF16)],
        [early, planes],
        flops=4 * rows * width * channels,
        place=place,
    )
    arrived = [
        lax.ppermute(
            partial,
            ("pipe", "tensor"),
            [(n + i, (i + s) % n) for i in range(n)] + [(i, n + i) for i in range(n)],
        )
        for s in range(n)
    ]
    all_early = swapped([early] * n, early_pairs)
    upstream, grad_scaled, payload = call(
        functools.partial(upstream_kernel, n),
        [
            shaped((rows, width), BF16),
            shaped((rows, channels), F32),
            shaped((n, CODE + rows + share, channels), BF16),
        ],
        [frame_counts, cotangent_flat, back_weight, normal, activated, shares, *arrived[::-1]],
        [table],
        smem=1,
        place=place,
        flops=2 * rows * width * channels,
    )
    late, total, late_parts, all_early = backward(0, grad_scaled, payload, [total], all_early)
    all_late = swapped([late] * n, over_dp_on(0))
    (payload,) = call(
        functools.partial(last_partial_kernel, n),
        [shaped((n, 2 * rows, channels), BF16)],
        [late, planes, *early_parts, *late_parts],
        [pltpu.VMEM((rows, width), BF16)],
        flops=4 * rows * width * channels,
        place=place,
    )
    moved = swapped(payload, over_tensor)
    (all_inputs,) = call(
        functools.partial(inputs_kernel, n),
        [shaped((channels, n * rows), BF16)],
        [*early_parts, *late_parts],
        [pltpu.VMEM((n, rows, channels), BF16)],
        place=place,
    )
    glu_grad, kernel_grad = call(
        functools.partial(glu_kernel, n),
        [shaped((channels, 2, channels), F32), taps_shape],
        [all_inputs, *all_early[::-1], *all_late[::-1]],
        flops=4 * rows * width * channels,
        place=place,
    )
    kernel_grad, *moved = tied(kernel_grad, *moved)
    input_grad, out_grad = call(
        functools.partial(out_kernel, n),
        [block_shape, shaped((channels, channels), F32)],
        [upstream, *moved[::-1], *early_parts, *late_parts],
        [pltpu.VMEM((n, rows, channels), BF16)],
        flops=2 * rows * width * channels,
        place=place,
    )
    return (
        input_grad.reshape(1, utterances, frames, channels),
        glu_grad[None],
        out_grad[None],
        kernel_grad[None],
        total[1:2],
        total[0:1],
    )


def solution(mesh):
    placed = (
        P("pipe", "dp", None, None),
        P("dp", None, None),
        P("dp"),
        P("pipe", None, None, "tensor"),
        P("pipe", None, "tensor"),
        P("pipe", "tensor"),
        P("pipe", "tensor"),
        P("pipe", None, "tensor"),
    )
    n = mesh.shape["dp"]
    paired = n == mesh.shape["tensor"] and n in (2, 4, 8) and mesh.shape["pipe"] == 2
    return jax.shard_map(
        paired_shards if paired else general_shards,
        mesh=mesh,
        in_specs=placed,
        out_specs=(
            P("pipe", "dp", None, "tensor"),
            P("pipe", "dp", None, "tensor"),
            P("pipe", "dp", "tensor"),
            P("pipe", None, "tensor"),
            P("pipe", "tensor"),
            P("pipe", "tensor"),
        ),
        check_vma=False,
    )
```

```python
import functools

import jax
import jax.numpy as jnp
from jax import lax
from jax.experimental import pallas as pl
from jax.experimental.pallas import tpu as pltpu
from jax.sharding import PartitionSpec as P

D = 1536
KERNEL = 32
LEFT = KERNEL // 2
EPSILON = 1e-05
MOST_PERMUTES = 8
LANES = 128
CODE = 16
VMEM_BYTES = 12 << 20
F32 = jnp.float32
BF16 = jnp.bfloat16
VMEM = pl.BlockSpec(memory_space=pltpu.VMEM)
SMEM = pl.BlockSpec(memory_space=pltpu.SMEM)


def shifted(shard, axis, by):
    devices = lax.axis_size(axis)
    pairs = [(i, i + by) for i in range(devices) if 0 <= i + by < devices]
    return lax.ppermute(shard, axis, pairs)


def depthwise(signal, taps, low_pad, high_pad, channels):
    return lax.conv_general_dilated(
        signal,
        taps[:, None, :],
        window_strides=(1,),
        padding=[(low_pad, high_pad)],
        dimension_numbers=("NWC", "WIO", "NWC"),
        feature_group_count=channels,
        precision=lax.Precision.HIGHEST,
    )


def general_shards(
    saved_inputs, cotangent, frame_counts, glu_weight, conv_kernel, norm_gain, norm_bias, out_weight
):
    channels = D // lax.axis_size("tensor")
    tensor_index = lax.axis_index("tensor")
    pipe_index = lax.axis_index("pipe")
    inputs = saved_inputs[0]
    utterances = inputs.shape[0]
    frames = inputs.shape[1]
    left_pad = KERNEL // 2
    positions = jnp.arange(frames, dtype=jnp.int32)
    validity = (positions[None, :] < frame_counts[:, None]).astype(jnp.float32)[..., None]
    glu_flat = glu_weight[0].reshape(D, 2 * channels)
    kernel_taps = conv_kernel[0]
    gain_local = norm_gain[0]
    bias_local = norm_bias[0]
    back_weight = out_weight[0]
    inputs_flat = inputs.reshape(-1, D)
    projected = jnp.dot(inputs_flat, glu_flat, preferred_element_type=jnp.float32).reshape(
        utterances, frames, 2, channels
    )
    gated = projected[:, :, 0] * jax.nn.sigmoid(projected[:, :, 1]) * validity
    convolved = depthwise(gated, kernel_taps, left_pad, KERNEL - 1 - left_pad, channels)
    moment_sums = lax.psum(
        (
            jnp.sum(convolved * validity, axis=(0, 1)),
            jnp.sum(convolved * convolved * validity, axis=(0, 1)),
            jnp.sum(validity),
        ),
        "dp",
    )
    frame_total = moment_sums[2]
    center = moment_sums[0] / frame_total
    inv_std = lax.rsqrt(moment_sums[1] / frame_total - center * center + EPSILON)
    normed = (convolved - center) * inv_std
    scaled = gain_local * normed + bias_local
    squash = jax.nn.sigmoid(scaled)
    activated = (scaled * squash * validity).astype(jnp.bfloat16)
    padded = jnp.pad(gated, ((0, 0), (left_pad, KERNEL - 1 - left_pad), (0, 0)))
    windows = jnp.stack([padded[:, tap_index : tap_index + frames] for tap_index in range(KERNEL)])
    validity_full = jnp.broadcast_to(validity, normed.shape)
    squash_b = jax.nn.sigmoid(projected[:, :, 1])

    def backward(upstream, with_weights):
        grad_act = jnp.dot(
            upstream.reshape(-1, D), back_weight, preferred_element_type=jnp.float32
        ).reshape(utterances, frames, channels)
        grad_scaled = grad_act * validity * squash * (1.0 + scaled * (1.0 - squash))
        stacked = jnp.stack([grad_scaled, validity_full, validity_full * normed])
        tap_sums = jnp.einsum("jutc,kutc->jkc", stacked, windows, precision=lax.Precision.HIGHEST)
        bias_grad, gain_grad, tap_sums = lax.psum(
            (
                jnp.sum(grad_scaled, axis=(0, 1)),
                jnp.sum(grad_scaled * normed, axis=(0, 1)),
                tap_sums,
            ),
            "dp",
        )
        factor = gain_local * inv_std
        grad_conv = (
            factor
            * (grad_scaled - bias_grad / frame_total - normed * gain_grad / frame_total)
            * validity
        )
        kernel_grad = factor * (
            tap_sums[0]
            - bias_grad / frame_total * tap_sums[1]
            - gain_grad / frame_total * tap_sums[2]
        )
        grad_gated = (
            depthwise(grad_conv, kernel_taps[::-1], KERNEL - 1 - left_pad, left_pad, channels)
            * validity
        )
        grad_proj = jnp.stack(
            [grad_gated * squash_b, grad_gated * projected[:, :, 0] * squash_b * (1.0 - squash_b)],
            axis=2,
        ).astype(jnp.bfloat16)
        grad_flat = grad_proj.reshape(-1, 2 * channels)
        reduced = lax.psum_scatter(
            lax.dot_general(
                glu_flat, grad_flat, (((1,), (1,)), ((), ())), preferred_element_type=jnp.float32
            ).astype(jnp.bfloat16),
            "tensor",
            scatter_dimension=0,
            tiled=True,
        ).astype(jnp.float32)
        upstream_part = lax.dynamic_slice_in_dim(upstream, tensor_index * channels, channels, 2)
        input_grad = (
            upstream_part.astype(jnp.float32) + reduced.T.reshape(utterances, frames, channels)
        ).astype(jnp.bfloat16)
        if not with_weights:
            return (input_grad, None)
        glu_grad = lax.dot_general(
            inputs_flat, grad_flat, (((0,), (0,)), ((), ())), preferred_element_type=jnp.float32
        ).reshape(1, D, 2, channels)
        out_grad = lax.dot_general(
            upstream.reshape(-1, D),
            activated.reshape(-1, channels),
            (((0,), (0,)), ((), ())),
            preferred_element_type=jnp.float32,
        ).reshape(1, D, channels)
        return (input_grad, (glu_grad, out_grad, kernel_grad, gain_grad, bias_grad))

    first_grad = backward(cotangent, False)[0]
    whole = lax.all_gather(first_grad, "tensor", axis=2, tiled=True)
    arrived = shifted(whole, "pipe", -1)
    upstream_now = jnp.where(pipe_index == 1, cotangent, arrived)
    final_grad, weight_parts = backward(upstream_now, True)
    input_grads = final_grad[None]
    glu_grad, out_grad, kernel_grad, gain_grad, bias_grad = weight_parts
    glu_shard, out_shard = (
        lax.psum_scatter(glu_grad, "dp", scatter_dimension=1, tiled=True),
        lax.psum_scatter(out_grad, "dp", scatter_dimension=1, tiled=True),
    )
    return (input_grads, glu_shard, out_shard, kernel_grad[None], gain_grad[None], bias_grad[None])


def swapped(parts, pairs_of):
    sizes = [lax.axis_size(axis) for axis in ("dp", "pipe", "tensor")]
    out = [parts[0]]
    for s in range(1, len(parts)):
        pairs = []
        for d in range(sizes[0]):
            for p in range(sizes[1]):
                for t in range(sizes[2]):
                    e, q, r = pairs_of(s, d, p, t)
                    here = (d * sizes[1] + p) * sizes[2] + t
                    pairs.append((here, (e * sizes[1] + q) * sizes[2] + r))
        out.append(lax.ppermute(parts[s], ("dp", "pipe", "tensor"), pairs))
    return out


def over_dp(s, d, p, t):
    return d ^ s, p, t


def over_tensor(s, d, p, t):
    return d, p, t ^ s


def over_dp_on(pipe):
    return lambda s, d, p, t: over_dp(s, d, p, t) if p == pipe else over_tensor(s, d, p, t)


def tied(first, *others):
    return lax.optimization_barrier((first, *others))


def early_pairs(s, d, p, t):
    if p == 1:
        return d ^ s, p, t
    return (d, p, t ^ 1) if s == 1 else (d ^ 1, p, t) if s == 2 else (d, p, t ^ 2)


def handing(packed, n):
    rows = packed.shape[0] - (packed.shape[0] - KERNEL) // 3
    return [packed, packed] + [packed[:rows]] * (n - 2)


def late_pairs(s, d, p, t):
    if p == 0:
        return d ^ s, p, t
    return (d, p, t ^ 1) if s == 1 else (d, p, t ^ 2)


def folded(parts):
    parts = list(parts)
    while len(parts) > 1:
        parts = [parts[i] + parts[i + 1] for i in range(0, len(parts), 2)]
    return parts[0]


def strips(channels):
    return [slice(low, min(low + LANES, channels)) for low in range(0, channels, LANES)]


def valid_rows(count, frames, lanes):
    rows = lax.broadcasted_iota(jnp.int32, (frames, lanes.stop - lanes.start), 0)
    return (rows < count).astype(F32)


def windows(padded, frames, lanes, offsets):
    for low in range(8):
        mine = [k for k in offsets if k % 8 == low]
        whole = padded[low : max(mine) + frames, lanes]
        for k in mine:
            yield k, whole[k - low : k - low + frames]


def cleared(padded, frames):
    padded[:LEFT, :] = jnp.zeros((LEFT, padded.shape[1]), F32)
    padded[LEFT + frames :, :] = jnp.zeros((padded.shape[0] - LEFT - frames, padded.shape[1]), F32)


def below(rows, block, size):
    return slice(rows.start + block * size, rows.stop + block * size)


def coded(sums, lines):
    value = sums[:lines, :]
    head = value.astype(BF16).astype(F32)
    middle = (value - head).astype(BF16).astype(F32)
    rest = value - head - middle
    blank = jnp.zeros((CODE - 3 * lines, value.shape[1]), F32)
    return jnp.concatenate([head, middle, rest, blank]).astype(BF16)


def decoded(ref, lines, lanes):
    value = ref[:CODE, lanes].astype(F32)
    return value[:lines] + value[lines : 2 * lines] + value[2 * lines : 3 * lines]


def column(index, s, channels):
    return pl.ds(pl.multiple_of((index ^ s) * channels, channels), channels)


def share_rows(place, share):
    return pl.ds(pl.multiple_of(place * share, share), share)


def forward_kernel(place, counts, projected, taps, inputs, kept, payload, padded, sums):
    utterances = counts.shape[0]
    size = projected.shape[1]
    frames, channels = size // utterances, projected.shape[2]
    share = payload.shape[1] - CODE
    cleared(padded, frames)
    sums[...] = jnp.zeros_like(sums)
    total = sum(counts[u] for u in range(utterances))
    sums[2:3, :] = jnp.full((1, channels), total, jnp.int32).astype(F32)
    kept[4 * size : 4 * size + KERNEL, :] = taps[...]
    for u in range(utterances):
        rows = slice(u * frames, (u + 1) * frames)
        for lanes in strips(channels):
            valid = valid_rows(counts[u], frames, lanes)
            linear = projected[0, rows, lanes]
            gate = jax.nn.sigmoid(projected[1, rows, lanes])
            value = linear * gate * valid
            kept[below(rows, 0, size), lanes] = linear
            kept[below(rows, 1, size), lanes] = gate
            kept[below(rows, 2, size), lanes] = value
            padded[LEFT : LEFT + frames, lanes] = value
            out = jnp.zeros_like(value)
            for k, window in windows(padded, frames, lanes, range(KERNEL)):
                out += taps[k : k + 1, lanes] * window
            kept[below(rows, 3, size), lanes] = out
            part = out * valid
            sums[0:1, lanes] += jnp.sum(part, axis=0, keepdims=True)
            sums[1:2, lanes] += jnp.sum(part * out, axis=0, keepdims=True)
    code = coded(sums, 3)
    for s in range(payload.shape[0]):
        payload[s, :CODE, :] = code
        payload[s, CODE:, :] = inputs[share_rows(place[1], share), column(place[0], s, channels)]


def scaled_sums(sums, u, lanes, grad_scaled, normed):
    rows = [
        jnp.sum(grad_scaled, axis=0, keepdims=True),
        jnp.sum(grad_scaled * normed, axis=0, keepdims=True),
    ]
    for i, row in enumerate(rows):
        if u == 0:
            sums[i : i + 1, lanes] = row
        else:
            sums[i : i + 1, lanes] += row


def filled(payload, small, place, sums, block, source, share):
    channels = payload.shape[2]
    size = block.shape[0]
    code = coded(sums, 2)
    small[:CODE, :] = code
    small[CODE:, :] = source[
        share_rows(place[1], share), column(place[0], payload.shape[0], channels)
    ]
    for s in range(payload.shape[0]):
        payload[s, :CODE, :] = code
        payload[s, CODE : CODE + size, :] = block[...]
        payload[s, CODE + size :, :] = source[
            share_rows(place[1], share), column(place[0], s, channels)
        ]


def block_of(parts, handed, i, size):
    if i + 1 < len(parts):
        return parts[i][CODE : CODE + size, :]
    return handed[handed.shape[0] - size :, :]


def norm_kernel(place, counts, kept, gain, bias, grad_act, cotangent, *refs):
    *moments, normal, activated, shares, payload, small, sums = refs
    moments = moments[::-1]
    utterances = counts.shape[0]
    size, channels = grad_act.shape
    frames = size // utterances
    share = size // len(moments)
    sums[...] = jnp.zeros_like(sums)
    for s, part in enumerate(moments):
        shares[s * share : (s + 1) * share, :] = part[CODE:, :]
    for lanes in strips(channels):
        moment = folded([decoded(part, 3, lanes) for part in moments])
        total = moment[2:3]
        center = moment[0:1] / total
        inv_std = lax.rsqrt(moment[1:2] / total - center * center + EPSILON)
        normal[3 * size : 3 * size + 1, lanes] = gain[:, lanes] * inv_std
        normal[3 * size + 1 : 3 * size + 2, lanes] = total
        for u in range(utterances):
            rows = slice(u * frames, (u + 1) * frames)
            valid = valid_rows(counts[u], frames, lanes)
            norm = (kept[below(rows, 3, size), lanes] - center) * inv_std
            scaled = gain[:, lanes] * norm + bias[:, lanes]
            squash = jax.nn.sigmoid(scaled)
            steep = valid * squash * (1.0 + scaled * (1.0 - squash))
            grad = grad_act[rows, lanes] * steep
            normal[below(rows, 0, size), lanes] = norm
            normal[below(rows, 1, size), lanes] = steep
            normal[below(rows, 2, size), lanes] = grad
            activated[rows, lanes] = (scaled * squash * valid).astype(BF16)
            scaled_sums(sums, u, lanes, grad, norm)

    @pl.when(place[2] == 1)
    def _():
        filled(payload, small, place, sums, activated, cotangent, share)

    @pl.when(place[2] == 0)
    def _():
        filled(payload, small, place, sums, shares, cotangent, share)


def upstream_kernel(
    parts, place, counts, cotangent, weight, normal, activated, shares, *refs
):
    arrived, (upstream, grad_scaled, payload, small, sums) = refs[:parts], refs[parts:]
    utterances = counts.shape[0]
    size, channels = grad_scaled.shape
    frames = size // utterances
    share = size // parts
    own = cotangent[...]
    total = own.astype(F32) + folded([part[...].astype(F32) for part in arrived])
    whole = jnp.where(place[2] == 1, own, total.astype(BF16))
    upstream[...] = whole
    grad_act = jnp.dot(whole, weight[...], preferred_element_type=F32)
    sums[...] = jnp.zeros_like(sums)
    for u in range(utterances):
        rows = slice(u * frames, (u + 1) * frames)
        for lanes in strips(channels):
            grad = grad_act[rows, lanes] * normal[below(rows, 1, size), lanes]
            grad_scaled[rows, lanes] = grad
            scaled_sums(sums, u, lanes, grad, normal[below(rows, 0, size), lanes])

    @pl.when(place[2] == 1)
    def _():
        filled(payload, small, place, sums, shares, upstream, share)

    @pl.when(place[2] == 0)
    def _():
        filled(payload, small, place, sums, activated, upstream, share)


def gate_kernel(parts, only_later, place, counts, grad_scaled, kept, normal, tap_table, *refs):
    sums, (grad_taps, *earlier, packed, totals_out, padded) = refs[:parts][::-1], refs[parts:]
    utterances = counts.shape[0]
    channels = packed.shape[1]
    size = (packed.shape[0] - KERNEL) // 3
    frames = size // utterances
    base = 2 * size if only_later else 0
    packed[2 * size + KERNEL :, :] = sums[-2][CODE : CODE + size, :]

    def run():
        cleared(padded, frames)
        total = folded([decoded(part, 2, slice(None)) for part in sums])
        for ref in earlier:
            total = jnp.where(place[2] == 1, ref[...], total)
        totals_out[...] = total
        for lanes in strips(channels):
            factor = normal[3 * size : 3 * size + 1, lanes]
            frame_total = normal[3 * size + 1 : 3 * size + 2, lanes]
            bias_part = totals_out[0:1, lanes] / frame_total
            gain_part = totals_out[1:2, lanes] / frame_total
            packed[2 * size : 2 * size + KERNEL, lanes] = (
                factor
                * (
                    grad_taps[:, lanes]
                    - bias_part * tap_table[KERNEL : 2 * KERNEL, lanes]
                    - gain_part * tap_table[:KERNEL, lanes]
                )
            ).astype(BF16)
            for u in range(utterances):
                rows = slice(u * frames, (u + 1) * frames)
                valid = valid_rows(counts[u], frames, lanes)
                grad = grad_scaled[base + rows.start : base + rows.stop, lanes]
                norm = normal[below(rows, 0, size), lanes]
                padded[LEFT : LEFT + frames, lanes] = (
                    factor * (grad - bias_part - norm * gain_part) * valid
                )
                out = jnp.zeros_like(valid)
                for k, window in windows(padded, frames, lanes, range(1, KERNEL + 1)):
                    tap = 4 * size + KERNEL - k
                    out += kept[tap : tap + 1, lanes] * window
                gate = kept[below(rows, 1, size), lanes]
                first = out * valid * gate
                second = first * kept[below(rows, 0, size), lanes] * (1.0 - gate)
                packed[rows, lanes] = first.astype(BF16)
                packed[below(rows, 1, size), lanes] = second.astype(BF16)

    if only_later:
        pl.when(place[2] == 1)(run)
    else:
        run()


def halves_product(packed, planes, size):
    return sum(
        lax.dot_general(
            packed[h * size : (h + 1) * size, :],
            planes[h],
            (((1,), (1,)), ((), ())),
            preferred_element_type=F32,
        )
        for h in range(2)
    )


def first_partial_kernel(place, packed, planes, partial):
    @pl.when(place[2] == 1)
    def _():
        partial[...] = halves_product(packed, planes, partial.shape[0]).astype(BF16)


def last_partial_kernel(parts, place, packed, planes, *refs):
    early, late, (payload, partial) = refs[:parts], refs[parts : 2 * parts], refs[2 * parts :]
    size = partial.shape[0]
    channels = payload.shape[2]
    share = size // parts
    partial[...] = halves_product(packed, planes, size).astype(BF16)
    for s in range(payload.shape[0]):
        payload[s, :size, :] = partial[:, column(place[1], s, channels)]
        for i in range(parts):
            rows = slice(early[i].shape[0] - share, early[i].shape[0])
            value = jnp.where(place[2] == 1, early[i][rows, :], late[i][rows, :])
            payload[s, size + i * share : size + (i + 1) * share, :] = value


def out_kernel(parts, place, upstream, *refs):
    moved, early, late = (refs[i * parts : (i + 1) * parts] for i in range(3))
    moved = moved[::-1]
    early_handed, late_handed, input_grad, out_grad, whole = refs[3 * parts :]
    size, channels = input_grad.shape
    share = size // parts
    total = folded([part[:size, :].astype(F32) for part in moved])
    own = upstream[:, column(place[1], 0, channels)]
    input_grad[...] = (own.astype(F32) + total).astype(BF16)
    for j, part in enumerate(moved):
        for i in range(parts):
            rows = slice(size + i * share, size + (i + 1) * share)
            whole[i, share_rows(place[1] ^ j, share), :] = part[rows, :]
    out_grad[...] = sum(
        lax.dot_general(
            whole[i],
            jnp.where(
                place[2] == 1,
                block_of(early, early_handed, i, size),
                block_of(late, late_handed, i, size),
            ),
            (((0,), (0,)), ((), ())),
            preferred_element_type=F32,
        )
        for i in range(parts)
    )


def inputs_kernel(parts, place, *refs):
    early, late, refs = refs[:parts], refs[parts : 2 * parts], refs[2 * parts :]
    early_handed, late_handed, turned, whole = refs
    size = whole.shape[1]
    share = size // parts
    for j in range(parts):
        value = jnp.where(
            place[2] == 1,
            block_of(late, late_handed, j, size),
            block_of(early, early_handed, j, size),
        )
        for i in range(parts):
            whole[i, share_rows(place[1] ^ j, share), :] = value[i * share : (i + 1) * share]
    for i in range(parts):
        turned[:, i * size : (i + 1) * size] = whole[i].astype(F32).T.astype(BF16)


def glu_kernel(parts, place, *refs):
    early, late, refs = refs[:parts], refs[parts : 2 * parts], refs[2 * parts :]
    inputs, glu_grad, kernel_grad = refs
    early, late = early[::-1], late[::-1]
    size = inputs.shape[1] // parts
    is_later = place[2] == 1
    tail = slice(2 * size, 2 * size + KERNEL)
    for h in range(2):
        rows = slice(h * size, (h + 1) * size)
        both = [jnp.where(is_later, b[rows, :], c[rows, :]) for b, c in zip(early, late)]
        glu_grad[:, h, :] = jnp.dot(
            inputs[...], jnp.concatenate(both), preferred_element_type=F32
        )
    kernel_grad[...] = folded(
        [
            jnp.where(is_later, b[tail, :], c[tail, :]).astype(F32)
            for b, c in zip(early, late)
        ]
    )


def tap_kernel(base, with_ones, counts, kept, signal, out, padded):
    utterances = counts.shape[0]
    frames, channels = padded.shape[0] - KERNEL, out.shape[1]
    size = utterances * frames
    cleared(padded, frames)
    for lanes in strips(channels):
        for u in range(utterances):
            rows = slice(u * frames, (u + 1) * frames)
            valid = valid_rows(counts[u], frames, lanes)
            padded[LEFT : LEFT + frames, lanes] = kept[below(rows, 2, size), lanes]
            factors = [signal[base + rows.start : base + rows.stop, lanes] * valid]
            factors += [valid] if with_ones else []
            for k, window in windows(padded, frames, lanes, range(KERNEL)):
                for i, factor in enumerate(factors):
                    row = jnp.sum(factor * window, axis=0, keepdims=True)
                    at = slice(i * KERNEL + k, i * KERNEL + k + 1)
                    if u == 0:
                        out[at, lanes] = row
                    else:
                        out[at, lanes] += row


def call(kernel, outs, operands, scratch=(), smem=0, flops=0, place=None):
    if place is not None:
        inner = kernel
        operands, smem = [*place, *operands], smem + len(place)

        def kernel(d, t, p, *refs):
            inner((d[0], t[0], p[0]), *refs)

    moved = sum(x.size * x.dtype.itemsize for x in operands)
    moved += sum(x.size * x.dtype.itemsize for x in outs)
    return pl.pallas_call(
        kernel,
        out_shape=outs,
        in_specs=[SMEM] * smem + [VMEM] * (len(operands) - smem),
        out_specs=[VMEM] * len(outs),
        scratch_shapes=list(scratch),
        compiler_params=pltpu.CompilerParams(vmem_limit_bytes=VMEM_BYTES),
        cost_estimate=pl.CostEstimate(flops=flops, bytes_accessed=moved, transcendentals=0),
    )(*operands)


def paired_shards(
    saved_inputs, cotangent, frame_counts, glu_weight, conv_kernel, norm_gain, norm_bias, out_weight
):
    inputs = saved_inputs[0]
    utterances, frames, width = inputs.shape
    channels = out_weight.shape[-1]
    rows = utterances * frames
    n = lax.axis_size("dp")
    share = rows // n
    place = [lax.axis_index(axis).astype(jnp.int32).reshape(1) for axis in ("dp", "tensor", "pipe")]
    weight = glu_weight[0]
    taps = conv_kernel[0]
    back_weight = out_weight[0]
    inputs_flat = inputs.reshape(rows, width)
    cotangent_flat = cotangent.reshape(rows, width)
    shaped = jax.ShapeDtypeStruct
    taps_shape = shaped((KERNEL, channels), F32)
    block_shape = shaped((rows, channels), BF16)
    padded = pltpu.VMEM((frames + KERNEL, channels), F32)
    table = pltpu.VMEM((8, channels), F32)
    conv_work = 2 * KERNEL * rows * channels

    def product(a, b, dims):
        return lax.dot_general(a, b, (dims, ((), ())), preferred_element_type=F32)

    projected = product(inputs_flat, weight, ((1,), (0,))).transpose(1, 0, 2)
    kept, payload = call(
        forward_kernel,
        [shaped((4 * rows + KERNEL, channels), F32), shaped((n, CODE + share, channels), BF16)],
        [frame_counts, projected, taps, inputs_flat],
        [padded, table],
        smem=1,
        place=place,
        flops=conv_work,
    )
    grad_act = product(cotangent_flat, back_weight, ((1,), (0,)))
    planes = weight.transpose(1, 0, 2)
    moments = swapped(payload, over_dp)
    normal, activated, shares, payload, small = call(
        norm_kernel,
        [
            shaped((3 * rows + 8, channels), F32),
            block_shape,
            block_shape,
            shaped((n - 1, CODE + rows + share, channels), BF16),
            shaped((CODE + share, channels), BF16),
        ],
        [frame_counts, kept, norm_gain, norm_bias, grad_act, cotangent_flat, *moments[::-1]],
        [table],
        smem=1,
        place=place,
    )

    def tap_sums(signal, base, with_ones):
        (out,) = call(
            functools.partial(tap_kernel, base, with_ones),
            [shaped((2 * KERNEL, channels), F32) if with_ones else taps_shape],
            [frame_counts, kept, signal],
            [padded],
            smem=1,
            flops=conv_work,
        )
        return out

    tap_table = tap_sums(normal, 0, True)

    def backward(pipe, grad_scaled, payload, earlier, others):
        parts = swapped(payload, over_dp_on(pipe))
        grad_taps = tap_sums(grad_scaled, 2 * rows if pipe == 1 else 0, False)
        grad_taps, *others = tied(grad_taps, *others)
        packed, total = call(
            functools.partial(gate_kernel, n, pipe == 1),
            [shaped((3 * rows + KERNEL, channels), BF16), shaped((2, channels), F32)],
            [frame_counts, grad_scaled, kept, normal, tap_table, *parts[::-1]]
            + [grad_taps, *earlier],
            [padded],
            smem=1,
            place=place,
            flops=conv_work,
        )
        return packed, total, parts, others

    early, total, early_parts, _ = backward(1, normal, [*payload, small], [], [])
    (partial,) = call(
        first_partial_kernel,
        [shaped((rows, width), BF16)],
        [early, planes],
        flops=4 * rows * width * channels,
        place=place,
    )
    arrived = [
        lax.ppermute(
            partial,
            ("pipe", "tensor"),
            [(n + i, (i + s) % n) for i in range(n)] + [(i, n + i) for i in range(n)],
        )
        for s in range(n)
    ]
    all_early = swapped(handing(early, n), early_pairs)
    upstream, grad_scaled, payload, small = call(
        functools.partial(upstream_kernel, n),
        [
            shaped((rows, width), BF16),
            shaped((rows, channels), F32),
            shaped((n - 1, CODE + rows + share, channels), BF16),
            shaped((CODE + share, channels), BF16),
        ],
        [frame_counts, cotangent_flat, back_weight, normal, activated, shares, *arrived[::-1]],
        [table],
        smem=1,
        place=place,
        flops=2 * rows * width * channels,
    )
    late, total, late_parts, all_early = backward(
        0, grad_scaled, [*payload, small], [total], all_early
    )
    all_late = swapped(handing(late, n), late_pairs)
    (payload,) = call(
        functools.partial(last_partial_kernel, n),
        [shaped((n, 2 * rows, channels), BF16)],
        [late, planes, *early_parts, *late_parts],
        [pltpu.VMEM((rows, width), BF16)],
        flops=4 * rows * width * channels,
        place=place,
    )
    moved = swapped(payload, over_tensor)
    (all_inputs,) = call(
        functools.partial(inputs_kernel, n),
        [shaped((channels, n * rows), BF16)],
        [*early_parts, *late_parts, all_early[1], all_late[1]],
        [pltpu.VMEM((n, rows, channels), BF16)],
        place=place,
    )
    glu_grad, kernel_grad = call(
        functools.partial(glu_kernel, n),
        [shaped((channels, 2, channels), F32), taps_shape],
        [*all_early[::-1], *all_late[::-1], all_inputs],
        flops=4 * rows * width * channels,
        place=place,
    )
    kernel_grad, *moved = tied(kernel_grad, *moved)
    input_grad, out_grad = call(
        functools.partial(out_kernel, n),
        [block_shape, shaped((channels, channels), F32)],
        [
            upstream,
            *moved[::-1],
            *early_parts,
            *late_parts,
            all_early[1],
            all_late[1],
        ],
        [pltpu.VMEM((n, rows, channels), BF16)],
        flops=2 * rows * width * channels,
        place=place,
    )
    return (
        input_grad.reshape(1, utterances, frames, channels),
        glu_grad[None],
        out_grad[None],
        kernel_grad[None],
        total[1:2],
        total[0:1],
    )


def solution(mesh):
    placed = (
        P("pipe", "dp", None, None),
        P("dp", None, None),
        P("dp"),
        P("pipe", None, None, "tensor"),
        P("pipe", None, "tensor"),
        P("pipe", "tensor"),
        P("pipe", "tensor"),
        P("pipe", None, "tensor"),
    )
    n = mesh.shape["dp"]
    paired = n == mesh.shape["tensor"] == 4 and mesh.shape["pipe"] == 2
    return jax.shard_map(
        paired_shards if paired else general_shards,
        mesh=mesh,
        in_specs=placed,
        out_specs=(
            P("pipe", "dp", None, "tensor"),
            P("pipe", "dp", None, "tensor"),
            P("pipe", "dp", "tensor"),
            P("pipe", None, "tensor"),
            P("pipe", "tensor"),
            P("pipe", "tensor"),
        ),
        check_vma=False,
    )
```

```python
import functools

import jax
import jax.numpy as jnp
from jax import lax
from jax.experimental import pallas as pl
from jax.experimental.pallas import tpu as pltpu
from jax.sharding import PartitionSpec as P

D = 1536
KERNEL = 32
LEFT = KERNEL // 2
EPSILON = 1e-05
MOST_PERMUTES = 8
LANES = 128
CODE = 16
VMEM_BYTES = 12 << 20
F32 = jnp.float32
BF16 = jnp.bfloat16
VMEM = pl.BlockSpec(memory_space=pltpu.VMEM)
SMEM = pl.BlockSpec(memory_space=pltpu.SMEM)


def shifted(shard, axis, by):
    devices = lax.axis_size(axis)
    pairs = [(i, i + by) for i in range(devices) if 0 <= i + by < devices]
    return lax.ppermute(shard, axis, pairs)


def depthwise(signal, taps, low_pad, high_pad, channels):
    return lax.conv_general_dilated(
        signal,
        taps[:, None, :],
        window_strides=(1,),
        padding=[(low_pad, high_pad)],
        dimension_numbers=("NWC", "WIO", "NWC"),
        feature_group_count=channels,
        precision=lax.Precision.HIGHEST,
    )


def general_shards(
    saved_inputs, cotangent, frame_counts, glu_weight, conv_kernel, norm_gain, norm_bias, out_weight
):
    channels = D // lax.axis_size("tensor")
    tensor_index = lax.axis_index("tensor")
    pipe_index = lax.axis_index("pipe")
    inputs = saved_inputs[0]
    utterances = inputs.shape[0]
    frames = inputs.shape[1]
    left_pad = KERNEL // 2
    positions = jnp.arange(frames, dtype=jnp.int32)
    validity = (positions[None, :] < frame_counts[:, None]).astype(jnp.float32)[..., None]
    glu_flat = glu_weight[0].reshape(D, 2 * channels)
    kernel_taps = conv_kernel[0]
    gain_local = norm_gain[0]
    bias_local = norm_bias[0]
    back_weight = out_weight[0]
    inputs_flat = inputs.reshape(-1, D)
    projected = jnp.dot(inputs_flat, glu_flat, preferred_element_type=jnp.float32).reshape(
        utterances, frames, 2, channels
    )
    gated = projected[:, :, 0] * jax.nn.sigmoid(projected[:, :, 1]) * validity
    convolved = depthwise(gated, kernel_taps, left_pad, KERNEL - 1 - left_pad, channels)
    moment_sums = lax.psum(
        (
            jnp.sum(convolved * validity, axis=(0, 1)),
            jnp.sum(convolved * convolved * validity, axis=(0, 1)),
            jnp.sum(validity),
        ),
        "dp",
    )
    frame_total = moment_sums[2]
    center = moment_sums[0] / frame_total
    inv_std = lax.rsqrt(moment_sums[1] / frame_total - center * center + EPSILON)
    normed = (convolved - center) * inv_std
    scaled = gain_local * normed + bias_local
    squash = jax.nn.sigmoid(scaled)
    activated = (scaled * squash * validity).astype(jnp.bfloat16)
    padded = jnp.pad(gated, ((0, 0), (left_pad, KERNEL - 1 - left_pad), (0, 0)))
    windows = jnp.stack([padded[:, tap_index : tap_index + frames] for tap_index in range(KERNEL)])
    validity_full = jnp.broadcast_to(validity, normed.shape)
    squash_b = jax.nn.sigmoid(projected[:, :, 1])

    def backward(upstream, with_weights):
        grad_act = jnp.dot(
            upstream.reshape(-1, D), back_weight, preferred_element_type=jnp.float32
        ).reshape(utterances, frames, channels)
        grad_scaled = grad_act * validity * squash * (1.0 + scaled * (1.0 - squash))
        stacked = jnp.stack([grad_scaled, validity_full, validity_full * normed])
        tap_sums = jnp.einsum("jutc,kutc->jkc", stacked, windows, precision=lax.Precision.HIGHEST)
        bias_grad, gain_grad, tap_sums = lax.psum(
            (
                jnp.sum(grad_scaled, axis=(0, 1)),
                jnp.sum(grad_scaled * normed, axis=(0, 1)),
                tap_sums,
            ),
            "dp",
        )
        factor = gain_local * inv_std
        grad_conv = (
            factor
            * (grad_scaled - bias_grad / frame_total - normed * gain_grad / frame_total)
            * validity
        )
        kernel_grad = factor * (
            tap_sums[0]
            - bias_grad / frame_total * tap_sums[1]
            - gain_grad / frame_total * tap_sums[2]
        )
        grad_gated = (
            depthwise(grad_conv, kernel_taps[::-1], KERNEL - 1 - left_pad, left_pad, channels)
            * validity
        )
        grad_proj = jnp.stack(
            [grad_gated * squash_b, grad_gated * projected[:, :, 0] * squash_b * (1.0 - squash_b)],
            axis=2,
        ).astype(jnp.bfloat16)
        grad_flat = grad_proj.reshape(-1, 2 * channels)
        reduced = lax.psum_scatter(
            lax.dot_general(
                glu_flat, grad_flat, (((1,), (1,)), ((), ())), preferred_element_type=jnp.float32
            ).astype(jnp.bfloat16),
            "tensor",
            scatter_dimension=0,
            tiled=True,
        ).astype(jnp.float32)
        upstream_part = lax.dynamic_slice_in_dim(upstream, tensor_index * channels, channels, 2)
        input_grad = (
            upstream_part.astype(jnp.float32) + reduced.T.reshape(utterances, frames, channels)
        ).astype(jnp.bfloat16)
        if not with_weights:
            return (input_grad, None)
        glu_grad = lax.dot_general(
            inputs_flat, grad_flat, (((0,), (0,)), ((), ())), preferred_element_type=jnp.float32
        ).reshape(1, D, 2, channels)
        out_grad = lax.dot_general(
            upstream.reshape(-1, D),
            activated.reshape(-1, channels),
            (((0,), (0,)), ((), ())),
            preferred_element_type=jnp.float32,
        ).reshape(1, D, channels)
        return (input_grad, (glu_grad, out_grad, kernel_grad, gain_grad, bias_grad))

    first_grad = backward(cotangent, False)[0]
    whole = lax.all_gather(first_grad, "tensor", axis=2, tiled=True)
    arrived = shifted(whole, "pipe", -1)
    upstream_now = jnp.where(pipe_index == 1, cotangent, arrived)
    final_grad, weight_parts = backward(upstream_now, True)
    input_grads = final_grad[None]
    glu_grad, out_grad, kernel_grad, gain_grad, bias_grad = weight_parts
    glu_shard, out_shard = (
        lax.psum_scatter(glu_grad, "dp", scatter_dimension=1, tiled=True),
        lax.psum_scatter(out_grad, "dp", scatter_dimension=1, tiled=True),
    )
    return (input_grads, glu_shard, out_shard, kernel_grad[None], gain_grad[None], bias_grad[None])


def swapped(parts, pairs_of):
    sizes = [lax.axis_size(axis) for axis in ("dp", "pipe", "tensor")]
    out = [parts[0]]
    for s in range(1, len(parts)):
        pairs = []
        for d in range(sizes[0]):
            for p in range(sizes[1]):
                for t in range(sizes[2]):
                    e, q, r = pairs_of(s, d, p, t)
                    here = (d * sizes[1] + p) * sizes[2] + t
                    pairs.append((here, (e * sizes[1] + q) * sizes[2] + r))
        out.append(lax.ppermute(parts[s], ("dp", "pipe", "tensor"), pairs))
    return out


def over_dp(s, d, p, t):
    return d ^ s, p, t


def over_tensor(s, d, p, t):
    return d, p, t ^ s


def over_dp_on(pipe):
    return lambda s, d, p, t: over_dp(s, d, p, t) if p == pipe else over_tensor(s, d, p, t)


def tied(first, *others):
    return lax.optimization_barrier((first, *others))


def early_pairs(s, d, p, t):
    if p == 1:
        return d ^ s, p, t
    return (d, p, t ^ 1) if s == 1 else (d ^ 1, p, t) if s == 2 else (d, p, t ^ 2)


def handing(packed, n):
    rows = packed.shape[0] - (packed.shape[0] - KERNEL) // 3
    return [packed, packed] + [packed[:rows]] * (n - 2)


def late_pairs(s, d, p, t):
    if p == 0:
        return d ^ s, p, t
    return (d, p, t ^ 1) if s == 1 else (d, p, t ^ 2)


def folded(parts):
    parts = list(parts)
    while len(parts) > 1:
        parts = [parts[i] + parts[i + 1] for i in range(0, len(parts), 2)]
    return parts[0]


def strips(channels):
    return [slice(low, min(low + LANES, channels)) for low in range(0, channels, LANES)]


def valid_rows(count, frames, lanes):
    rows = lax.broadcasted_iota(jnp.int32, (frames, lanes.stop - lanes.start), 0)
    return (rows < count).astype(F32)


def windows(padded, frames, lanes, offsets):
    for low in range(8):
        mine = [k for k in offsets if k % 8 == low]
        whole = padded[low : max(mine) + frames, lanes]
        for k in mine:
            yield k, whole[k - low : k - low + frames]


def cleared(padded, frames):
    padded[:LEFT, :] = jnp.zeros((LEFT, padded.shape[1]), F32)
    padded[LEFT + frames :, :] = jnp.zeros((padded.shape[0] - LEFT - frames, padded.shape[1]), F32)


def below(rows, block, size):
    return slice(rows.start + block * size, rows.stop + block * size)


def coded(sums, lines):
    value = sums[:lines, :]
    head = value.astype(BF16).astype(F32)
    middle = (value - head).astype(BF16).astype(F32)
    rest = value - head - middle
    blank = jnp.zeros((CODE - 3 * lines, value.shape[1]), F32)
    return jnp.concatenate([head, middle, rest, blank]).astype(BF16)


def decoded(ref, lines, lanes):
    value = ref[:CODE, lanes].astype(F32)
    return value[:lines] + value[lines : 2 * lines] + value[2 * lines : 3 * lines]


def column(index, s, channels):
    return pl.ds(pl.multiple_of((index ^ s) * channels, channels), channels)


def share_rows(place, share):
    return pl.ds(pl.multiple_of(place * share, share), share)


def forward_kernel(place, counts, projected, taps, inputs, kept, payload, padded, sums):
    utterances = counts.shape[0]
    size = projected.shape[1]
    frames, channels = size // utterances, projected.shape[2]
    share = payload.shape[1] - CODE
    cleared(padded, frames)
    sums[...] = jnp.zeros_like(sums)
    total = sum(counts[u] for u in range(utterances))
    sums[2:3, :] = jnp.full((1, channels), total, jnp.int32).astype(F32)
    kept[4 * size : 4 * size + KERNEL, :] = taps[...]
    for u in range(utterances):
        rows = slice(u * frames, (u + 1) * frames)
        for lanes in strips(channels):
            valid = valid_rows(counts[u], frames, lanes)
            linear = projected[0, rows, lanes]
            gate = jax.nn.sigmoid(projected[1, rows, lanes])
            value = linear * gate * valid
            kept[below(rows, 0, size), lanes] = linear
            kept[below(rows, 1, size), lanes] = gate
            kept[below(rows, 2, size), lanes] = value
            padded[LEFT : LEFT + frames, lanes] = value
            out = jnp.zeros_like(value)
            for k, window in windows(padded, frames, lanes, range(KERNEL)):
                out += taps[k : k + 1, lanes] * window
            kept[below(rows, 3, size), lanes] = out
            part = out * valid
            sums[0:1, lanes] += jnp.sum(part, axis=0, keepdims=True)
            sums[1:2, lanes] += jnp.sum(part * out, axis=0, keepdims=True)
    code = coded(sums, 3)
    for s in range(payload.shape[0]):
        payload[s, :CODE, :] = code
        payload[s, CODE:, :] = inputs[share_rows(place[1], share), column(place[0], s, channels)]


def scaled_sums(sums, u, lanes, grad_scaled, normed):
    rows = [
        jnp.sum(grad_scaled, axis=0, keepdims=True),
        jnp.sum(grad_scaled * normed, axis=0, keepdims=True),
    ]
    for i, row in enumerate(rows):
        if u == 0:
            sums[i : i + 1, lanes] = row
        else:
            sums[i : i + 1, lanes] += row


def filled(payload, small, place, sums, block, source, share):
    channels = payload.shape[2]
    size = block.shape[0]
    code = coded(sums, 2)
    small[:CODE, :] = code
    small[CODE:, :] = source[
        share_rows(place[1], share), column(place[0], payload.shape[0], channels)
    ]
    for s in range(payload.shape[0]):
        payload[s, :CODE, :] = code
        payload[s, CODE : CODE + size, :] = block[...]
        payload[s, CODE + size :, :] = source[
            share_rows(place[1], share), column(place[0], s, channels)
        ]


def block_of(parts, handed, i, size):
    if i + 1 < len(parts):
        return parts[i][CODE : CODE + size, :]
    return handed[handed.shape[0] - size :, :]


def norm_kernel(place, counts, kept, gain, bias, grad_act, cotangent, *refs):
    *moments, normal, activated, shares, payload, small, sums = refs
    moments = moments[::-1]
    utterances = counts.shape[0]
    size, channels = grad_act.shape
    frames = size // utterances
    share = size // len(moments)
    sums[...] = jnp.zeros_like(sums)
    for s, part in enumerate(moments):
        shares[s * share : (s + 1) * share, :] = part[CODE:, :]
    for lanes in strips(channels):
        moment = folded([decoded(part, 3, lanes) for part in moments])
        total = moment[2:3]
        center = moment[0:1] / total
        inv_std = lax.rsqrt(moment[1:2] / total - center * center + EPSILON)
        normal[3 * size : 3 * size + 1, lanes] = gain[:, lanes] * inv_std
        normal[3 * size + 1 : 3 * size + 2, lanes] = total
        for u in range(utterances):
            rows = slice(u * frames, (u + 1) * frames)
            valid = valid_rows(counts[u], frames, lanes)
            norm = (kept[below(rows, 3, size), lanes] - center) * inv_std
            scaled = gain[:, lanes] * norm + bias[:, lanes]
            squash = jax.nn.sigmoid(scaled)
            steep = valid * squash * (1.0 + scaled * (1.0 - squash))
            grad = grad_act[rows, lanes] * steep
            normal[below(rows, 0, size), lanes] = norm
            normal[below(rows, 1, size), lanes] = steep
            normal[below(rows, 2, size), lanes] = grad
            activated[rows, lanes] = (scaled * squash * valid).astype(BF16)
            scaled_sums(sums, u, lanes, grad, norm)

    @pl.when(place[2] == 1)
    def _():
        filled(payload, small, place, sums, activated, cotangent, share)

    @pl.when(place[2] == 0)
    def _():
        filled(payload, small, place, sums, shares, cotangent, share)


def upstream_kernel(
    parts, place, counts, cotangent, weight, normal, activated, shares, *refs
):
    arrived, (upstream, grad_scaled, payload, small, sums) = refs[:parts], refs[parts:]
    utterances = counts.shape[0]
    size, channels = grad_scaled.shape
    frames = size // utterances
    share = size // parts
    own = cotangent[...]
    total = own.astype(F32) + folded([part[...].astype(F32) for part in arrived])
    whole = jnp.where(place[2] == 1, own, total.astype(BF16))
    upstream[...] = whole
    grad_act = jnp.dot(whole, weight[...], preferred_element_type=F32)
    sums[...] = jnp.zeros_like(sums)
    for u in range(utterances):
        rows = slice(u * frames, (u + 1) * frames)
        for lanes in strips(channels):
            grad = grad_act[rows, lanes] * normal[below(rows, 1, size), lanes]
            grad_scaled[rows, lanes] = grad
            scaled_sums(sums, u, lanes, grad, normal[below(rows, 0, size), lanes])

    @pl.when(place[2] == 1)
    def _():
        filled(payload, small, place, sums, shares, upstream, share)

    @pl.when(place[2] == 0)
    def _():
        filled(payload, small, place, sums, activated, upstream, share)


def gate_kernel(parts, only_later, place, counts, grad_scaled, kept, normal, tap_table, *refs):
    sums, (grad_taps, *earlier, packed, totals_out, padded) = refs[:parts][::-1], refs[parts:]
    utterances = counts.shape[0]
    channels = packed.shape[1]
    size = (packed.shape[0] - KERNEL) // 3
    frames = size // utterances
    base = 2 * size if only_later else 0
    packed[2 * size + KERNEL :, :] = sums[-2][CODE : CODE + size, :]

    def run():
        cleared(padded, frames)
        total = folded([decoded(part, 2, slice(None)) for part in sums])
        for ref in earlier:
            total = jnp.where(place[2] == 1, ref[...], total)
        totals_out[...] = total
        for lanes in strips(channels):
            factor = normal[3 * size : 3 * size + 1, lanes]
            frame_total = normal[3 * size + 1 : 3 * size + 2, lanes]
            bias_part = totals_out[0:1, lanes] / frame_total
            gain_part = totals_out[1:2, lanes] / frame_total
            packed[2 * size : 2 * size + KERNEL, lanes] = (
                factor
                * (
                    grad_taps[:, lanes]
                    - bias_part * tap_table[KERNEL : 2 * KERNEL, lanes]
                    - gain_part * tap_table[:KERNEL, lanes]
                )
            ).astype(BF16)
            for u in range(utterances):
                rows = slice(u * frames, (u + 1) * frames)
                valid = valid_rows(counts[u], frames, lanes)
                grad = grad_scaled[base + rows.start : base + rows.stop, lanes]
                norm = normal[below(rows, 0, size), lanes]
                padded[LEFT : LEFT + frames, lanes] = (
                    factor * (grad - bias_part - norm * gain_part) * valid
                )
                out = jnp.zeros_like(valid)
                for k, window in windows(padded, frames, lanes, range(1, KERNEL + 1)):
                    tap = 4 * size + KERNEL - k
                    out += kept[tap : tap + 1, lanes] * window
                gate = kept[below(rows, 1, size), lanes]
                first = out * valid * gate
                second = first * kept[below(rows, 0, size), lanes] * (1.0 - gate)
                packed[rows, lanes] = first.astype(BF16)
                packed[below(rows, 1, size), lanes] = second.astype(BF16)

    if only_later:
        pl.when(place[2] == 1)(run)
    else:
        run()


def halves_product(packed, planes, size):
    return sum(
        lax.dot_general(
            packed[h * size : (h + 1) * size, :],
            planes[h],
            (((1,), (1,)), ((), ())),
            preferred_element_type=F32,
        )
        for h in range(2)
    )


def first_partial_kernel(place, packed, planes, partial):
    @pl.when(place[2] == 1)
    def _():
        partial[...] = halves_product(packed, planes, partial.shape[0]).astype(BF16)


def last_partial_kernel(parts, place, packed, planes, *refs):
    early, late, (payload, partial) = refs[:parts], refs[parts : 2 * parts], refs[2 * parts :]
    size = partial.shape[0]
    channels = payload.shape[2]
    share = size // parts
    partial[...] = halves_product(packed, planes, size).astype(BF16)
    for s in range(payload.shape[0]):
        payload[s, :size, :] = partial[:, column(place[1], s, channels)]
        for i in range(parts):
            rows = slice(early[i].shape[0] - share, early[i].shape[0])
            value = jnp.where(place[2] == 1, early[i][rows, :], late[i][rows, :])
            payload[s, size + i * share : size + (i + 1) * share, :] = value


def out_kernel(parts, place, upstream, *refs):
    moved, early, late = (refs[i * parts : (i + 1) * parts] for i in range(3))
    moved = moved[::-1]
    early_handed, late_handed, input_grad, out_grad, whole = refs[3 * parts :]
    size, channels = input_grad.shape
    share = size // parts
    total = folded([part[:size, :].astype(F32) for part in moved])
    own = upstream[:, column(place[1], 0, channels)]
    input_grad[...] = (own.astype(F32) + total).astype(BF16)
    for j, part in enumerate(moved):
        for i in range(parts):
            rows = slice(size + i * share, size + (i + 1) * share)
            whole[i, share_rows(place[1] ^ j, share), :] = part[rows, :]
    out_grad[...] = sum(
        lax.dot_general(
            whole[i],
            jnp.where(
                place[2] == 1,
                block_of(early, early_handed, i, size),
                block_of(late, late_handed, i, size),
            ),
            (((0,), (0,)), ((), ())),
            preferred_element_type=F32,
        )
        for i in range(parts)
    )


def inputs_kernel(parts, place, *refs):
    early, late, refs = refs[:parts], refs[parts : 2 * parts], refs[2 * parts :]
    early_handed, late_handed, turned, whole = refs
    size = whole.shape[1]
    share = size // parts
    for j in range(parts):
        value = jnp.where(
            place[2] == 1,
            block_of(late, late_handed, j, size),
            block_of(early, early_handed, j, size),
        )
        for i in range(parts):
            whole[i, share_rows(place[1] ^ j, share), :] = value[i * share : (i + 1) * share]
    for i in range(parts):
        turned[:, i * size : (i + 1) * size] = whole[i].astype(F32).T.astype(BF16)


def glu_kernel(parts, place, *refs):
    early, late, refs = refs[:parts], refs[parts : 2 * parts], refs[2 * parts :]
    inputs, glu_grad, kernel_grad = refs
    early, late = early[::-1], late[::-1]
    size = inputs.shape[1] // parts
    is_later = place[2] == 1
    tail = slice(2 * size, 2 * size + KERNEL)
    for h in range(2):
        rows = slice(h * size, (h + 1) * size)
        both = [jnp.where(is_later, b[rows, :], c[rows, :]) for b, c in zip(early, late)]
        glu_grad[:, h, :] = jnp.dot(
            inputs[...], jnp.concatenate(both), preferred_element_type=F32
        )
    kernel_grad[...] = folded(
        [
            jnp.where(is_later, b[tail, :], c[tail, :]).astype(F32)
            for b, c in zip(early, late)
        ]
    )


def last_kernel(parts, place, *refs):
    first, refs = refs[: 2 * parts + 1], refs[2 * parts + 1 :]
    second, (glu_grad, kernel_grad, *outs) = refs[: 3 * parts + 1], refs[3 * parts + 1 :]
    glu_kernel(parts, place, *first, glu_grad, kernel_grad)
    out_kernel(parts, place, *second, first[parts - 2], first[2 * parts - 2], *outs)


def tap_kernel(base, with_ones, counts, kept, signal, out, padded):
    utterances = counts.shape[0]
    frames, channels = padded.shape[0] - KERNEL, out.shape[1]
    size = utterances * frames
    cleared(padded, frames)
    for lanes in strips(channels):
        for u in range(utterances):
            rows = slice(u * frames, (u + 1) * frames)
            valid = valid_rows(counts[u], frames, lanes)
            padded[LEFT : LEFT + frames, lanes] = kept[below(rows, 2, size), lanes]
            factors = [signal[base + rows.start : base + rows.stop, lanes] * valid]
            factors += [valid] if with_ones else []
            for k, window in windows(padded, frames, lanes, range(KERNEL)):
                for i, factor in enumerate(factors):
                    row = jnp.sum(factor * window, axis=0, keepdims=True)
                    at = slice(i * KERNEL + k, i * KERNEL + k + 1)
                    if u == 0:
                        out[at, lanes] = row
                    else:
                        out[at, lanes] += row


def call(kernel, outs, operands, scratch=(), smem=0, flops=0, place=None):
    if place is not None:
        inner = kernel
        operands, smem = [*place, *operands], smem + len(place)

        def kernel(d, t, p, *refs):
            inner((d[0], t[0], p[0]), *refs)

    moved = sum(x.size * x.dtype.itemsize for x in operands)
    moved += sum(x.size * x.dtype.itemsize for x in outs)
    return pl.pallas_call(
        kernel,
        out_shape=outs,
        in_specs=[SMEM] * smem + [VMEM] * (len(operands) - smem),
        out_specs=[VMEM] * len(outs),
        scratch_shapes=list(scratch),
        compiler_params=pltpu.CompilerParams(vmem_limit_bytes=VMEM_BYTES),
        cost_estimate=pl.CostEstimate(flops=flops, bytes_accessed=moved, transcendentals=0),
    )(*operands)


def paired_shards(
    saved_inputs, cotangent, frame_counts, glu_weight, conv_kernel, norm_gain, norm_bias, out_weight
):
    inputs = saved_inputs[0]
    utterances, frames, width = inputs.shape
    channels = out_weight.shape[-1]
    rows = utterances * frames
    n = lax.axis_size("dp")
    share = rows // n
    place = [lax.axis_index(axis).astype(jnp.int32).reshape(1) for axis in ("dp", "tensor", "pipe")]
    weight = glu_weight[0]
    taps = conv_kernel[0]
    back_weight = out_weight[0]
    inputs_flat = inputs.reshape(rows, width)
    cotangent_flat = cotangent.reshape(rows, width)
    shaped = jax.ShapeDtypeStruct
    taps_shape = shaped((KERNEL, channels), F32)
    block_shape = shaped((rows, channels), BF16)
    padded = pltpu.VMEM((frames + KERNEL, channels), F32)
    table = pltpu.VMEM((8, channels), F32)
    conv_work = 2 * KERNEL * rows * channels

    def product(a, b, dims):
        return lax.dot_general(a, b, (dims, ((), ())), preferred_element_type=F32)

    projected = product(inputs_flat, weight, ((1,), (0,))).transpose(1, 0, 2)
    kept, payload = call(
        forward_kernel,
        [shaped((4 * rows + KERNEL, channels), F32), shaped((n, CODE + share, channels), BF16)],
        [frame_counts, projected, taps, inputs_flat],
        [padded, table],
        smem=1,
        place=place,
        flops=conv_work,
    )
    grad_act = product(cotangent_flat, back_weight, ((1,), (0,)))
    planes = weight.transpose(1, 0, 2)
    moments = swapped(payload, over_dp)
    normal, activated, shares, payload, small = call(
        norm_kernel,
        [
            shaped((3 * rows + 8, channels), F32),
            block_shape,
            block_shape,
            shaped((n - 1, CODE + rows + share, channels), BF16),
            shaped((CODE + share, channels), BF16),
        ],
        [frame_counts, kept, norm_gain, norm_bias, grad_act, cotangent_flat, *moments[::-1]],
        [table],
        smem=1,
        place=place,
    )

    def tap_sums(signal, base, with_ones):
        (out,) = call(
            functools.partial(tap_kernel, base, with_ones),
            [shaped((2 * KERNEL, channels), F32) if with_ones else taps_shape],
            [frame_counts, kept, signal],
            [padded],
            smem=1,
            flops=conv_work,
        )
        return out

    tap_table = tap_sums(normal, 0, True)

    def backward(pipe, grad_scaled, payload, earlier, others):
        parts = swapped(payload, over_dp_on(pipe))
        grad_taps = tap_sums(grad_scaled, 2 * rows if pipe == 1 else 0, False)
        grad_taps, *others = tied(grad_taps, *others)
        packed, total = call(
            functools.partial(gate_kernel, n, pipe == 1),
            [shaped((3 * rows + KERNEL, channels), BF16), shaped((2, channels), F32)],
            [frame_counts, grad_scaled, kept, normal, tap_table, *parts[::-1]]
            + [grad_taps, *earlier],
            [padded],
            smem=1,
            place=place,
            flops=conv_work,
        )
        return packed, total, parts, others

    early, total, early_parts, _ = backward(1, normal, [*payload, small], [], [])
    (partial,) = call(
        first_partial_kernel,
        [shaped((rows, width), BF16)],
        [early, planes],
        flops=4 * rows * width * channels,
        place=place,
    )
    arrived = [
        lax.ppermute(
            partial,
            ("pipe", "tensor"),
            [(n + i, (i + s) % n) for i in range(n)] + [(i, n + i) for i in range(n)],
        )
        for s in range(n)
    ]
    all_early = swapped(handing(early, n), early_pairs)
    upstream, grad_scaled, payload, small = call(
        functools.partial(upstream_kernel, n),
        [
            shaped((rows, width), BF16),
            shaped((rows, channels), F32),
            shaped((n - 1, CODE + rows + share, channels), BF16),
            shaped((CODE + share, channels), BF16),
        ],
        [frame_counts, cotangent_flat, back_weight, normal, activated, shares, *arrived[::-1]],
        [table],
        smem=1,
        place=place,
        flops=2 * rows * width * channels,
    )
    late, total, late_parts, all_early = backward(
        0, grad_scaled, [*payload, small], [total], all_early
    )
    all_late = swapped(handing(late, n), late_pairs)
    (payload,) = call(
        functools.partial(last_partial_kernel, n),
        [shaped((n, 2 * rows, channels), BF16)],
        [late, planes, *early_parts, *late_parts],
        [pltpu.VMEM((rows, width), BF16)],
        flops=4 * rows * width * channels,
        place=place,
    )
    moved = swapped(payload, over_tensor)
    (all_inputs,) = call(
        functools.partial(inputs_kernel, n),
        [shaped((channels, n * rows), BF16)],
        [*early_parts, *late_parts, all_early[1], all_late[1]],
        [pltpu.VMEM((n, rows, channels), BF16)],
        place=place,
    )
    glu_grad, kernel_grad, input_grad, out_grad = call(
        functools.partial(last_kernel, n),
        [
            shaped((channels, 2, channels), F32),
            taps_shape,
            block_shape,
            shaped((channels, channels), F32),
        ],
        [
            *all_early[::-1],
            *all_late[::-1],
            all_inputs,
            upstream,
            *moved[::-1],
            *early_parts,
            *late_parts,
        ],
        [pltpu.VMEM((n, rows, channels), BF16)],
        flops=6 * rows * width * channels,
        place=place,
    )
    return (
        input_grad.reshape(1, utterances, frames, channels),
        glu_grad[None],
        out_grad[None],
        kernel_grad[None],
        total[1:2],
        total[0:1],
    )


def solution(mesh):
    placed = (
        P("pipe", "dp", None, None),
        P("dp", None, None),
        P("dp"),
        P("pipe", None, None, "tensor"),
        P("pipe", None, "tensor"),
        P("pipe", "tensor"),
        P("pipe", "tensor"),
        P("pipe", None, "tensor"),
    )
    n = mesh.shape["dp"]
    paired = n == mesh.shape["tensor"] == 4 and mesh.shape["pipe"] == 2
    return jax.shard_map(
        paired_shards if paired else general_shards,
        mesh=mesh,
        in_specs=placed,
        out_specs=(
            P("pipe", "dp", None, "tensor"),
            P("pipe", "dp", None, "tensor"),
            P("pipe", "dp", "tensor"),
            P("pipe", None, "tensor"),
            P("pipe", "tensor"),
            P("pipe", "tensor"),
        ),
        check_vma=False,
    )
```

```python
import functools

import jax
import jax.numpy as jnp
from jax import lax
from jax.experimental import pallas as pl
from jax.experimental.pallas import tpu as pltpu
from jax.sharding import PartitionSpec as P

D = 1536
KERNEL = 32
LEFT = KERNEL // 2
EPSILON = 1e-05
MOST_PERMUTES = 8
LANES = 128
CODE = 16
VMEM_BYTES = 12 << 20
F32 = jnp.float32
BF16 = jnp.bfloat16
VMEM = pl.BlockSpec(memory_space=pltpu.VMEM)
SMEM = pl.BlockSpec(memory_space=pltpu.SMEM)


def shifted(shard, axis, by):
    devices = lax.axis_size(axis)
    pairs = [(i, i + by) for i in range(devices) if 0 <= i + by < devices]
    return lax.ppermute(shard, axis, pairs)


def depthwise(signal, taps, low_pad, high_pad, channels):
    return lax.conv_general_dilated(
        signal,
        taps[:, None, :],
        window_strides=(1,),
        padding=[(low_pad, high_pad)],
        dimension_numbers=("NWC", "WIO", "NWC"),
        feature_group_count=channels,
        precision=lax.Precision.HIGHEST,
    )


def general_shards(
    saved_inputs, cotangent, frame_counts, glu_weight, conv_kernel, norm_gain, norm_bias, out_weight
):
    channels = D // lax.axis_size("tensor")
    tensor_index = lax.axis_index("tensor")
    pipe_index = lax.axis_index("pipe")
    inputs = saved_inputs[0]
    utterances = inputs.shape[0]
    frames = inputs.shape[1]
    left_pad = KERNEL // 2
    positions = jnp.arange(frames, dtype=jnp.int32)
    validity = (positions[None, :] < frame_counts[:, None]).astype(jnp.float32)[..., None]
    glu_flat = glu_weight[0].reshape(D, 2 * channels)
    kernel_taps = conv_kernel[0]
    gain_local = norm_gain[0]
    bias_local = norm_bias[0]
    back_weight = out_weight[0]
    inputs_flat = inputs.reshape(-1, D)
    projected = jnp.dot(inputs_flat, glu_flat, preferred_element_type=jnp.float32).reshape(
        utterances, frames, 2, channels
    )
    gated = projected[:, :, 0] * jax.nn.sigmoid(projected[:, :, 1]) * validity
    convolved = depthwise(gated, kernel_taps, left_pad, KERNEL - 1 - left_pad, channels)
    moment_sums = lax.psum(
        (
            jnp.sum(convolved * validity, axis=(0, 1)),
            jnp.sum(convolved * convolved * validity, axis=(0, 1)),
            jnp.sum(validity),
        ),
        "dp",
    )
    frame_total = moment_sums[2]
    center = moment_sums[0] / frame_total
    inv_std = lax.rsqrt(moment_sums[1] / frame_total - center * center + EPSILON)
    normed = (convolved - center) * inv_std
    scaled = gain_local * normed + bias_local
    squash = jax.nn.sigmoid(scaled)
    activated = (scaled * squash * validity).astype(jnp.bfloat16)
    padded = jnp.pad(gated, ((0, 0), (left_pad, KERNEL - 1 - left_pad), (0, 0)))
    windows = jnp.stack([padded[:, tap_index : tap_index + frames] for tap_index in range(KERNEL)])
    validity_full = jnp.broadcast_to(validity, normed.shape)
    squash_b = jax.nn.sigmoid(projected[:, :, 1])

    def backward(upstream, with_weights):
        grad_act = jnp.dot(
            upstream.reshape(-1, D), back_weight, preferred_element_type=jnp.float32
        ).reshape(utterances, frames, channels)
        grad_scaled = grad_act * validity * squash * (1.0 + scaled * (1.0 - squash))
        stacked = jnp.stack([grad_scaled, validity_full, validity_full * normed])
        tap_sums = jnp.einsum("jutc,kutc->jkc", stacked, windows, precision=lax.Precision.HIGHEST)
        bias_grad, gain_grad, tap_sums = lax.psum(
            (
                jnp.sum(grad_scaled, axis=(0, 1)),
                jnp.sum(grad_scaled * normed, axis=(0, 1)),
                tap_sums,
            ),
            "dp",
        )
        factor = gain_local * inv_std
        grad_conv = (
            factor
            * (grad_scaled - bias_grad / frame_total - normed * gain_grad / frame_total)
            * validity
        )
        kernel_grad = factor * (
            tap_sums[0]
            - bias_grad / frame_total * tap_sums[1]
            - gain_grad / frame_total * tap_sums[2]
        )
        grad_gated = (
            depthwise(grad_conv, kernel_taps[::-1], KERNEL - 1 - left_pad, left_pad, channels)
            * validity
        )
        grad_proj = jnp.stack(
            [grad_gated * squash_b, grad_gated * projected[:, :, 0] * squash_b * (1.0 - squash_b)],
            axis=2,
        ).astype(jnp.bfloat16)
        grad_flat = grad_proj.reshape(-1, 2 * channels)
        reduced = lax.psum_scatter(
            lax.dot_general(
                glu_flat, grad_flat, (((1,), (1,)), ((), ())), preferred_element_type=jnp.float32
            ).astype(jnp.bfloat16),
            "tensor",
            scatter_dimension=0,
            tiled=True,
        ).astype(jnp.float32)
        upstream_part = lax.dynamic_slice_in_dim(upstream, tensor_index * channels, channels, 2)
        input_grad = (
            upstream_part.astype(jnp.float32) + reduced.T.reshape(utterances, frames, channels)
        ).astype(jnp.bfloat16)
        if not with_weights:
            return (input_grad, None)
        glu_grad = lax.dot_general(
            inputs_flat, grad_flat, (((0,), (0,)), ((), ())), preferred_element_type=jnp.float32
        ).reshape(1, D, 2, channels)
        out_grad = lax.dot_general(
            upstream.reshape(-1, D),
            activated.reshape(-1, channels),
            (((0,), (0,)), ((), ())),
            preferred_element_type=jnp.float32,
        ).reshape(1, D, channels)
        return (input_grad, (glu_grad, out_grad, kernel_grad, gain_grad, bias_grad))

    first_grad = backward(cotangent, False)[0]
    whole = lax.all_gather(first_grad, "tensor", axis=2, tiled=True)
    arrived = shifted(whole, "pipe", -1)
    upstream_now = jnp.where(pipe_index == 1, cotangent, arrived)
    final_grad, weight_parts = backward(upstream_now, True)
    input_grads = final_grad[None]
    glu_grad, out_grad, kernel_grad, gain_grad, bias_grad = weight_parts
    glu_shard, out_shard = (
        lax.psum_scatter(glu_grad, "dp", scatter_dimension=1, tiled=True),
        lax.psum_scatter(out_grad, "dp", scatter_dimension=1, tiled=True),
    )
    return (input_grads, glu_shard, out_shard, kernel_grad[None], gain_grad[None], bias_grad[None])


def swapped(parts, pairs_of):
    sizes = [lax.axis_size(axis) for axis in ("dp", "pipe", "tensor")]
    out = [parts[0]]
    for s in range(1, len(parts)):
        pairs = []
        for d in range(sizes[0]):
            for p in range(sizes[1]):
                for t in range(sizes[2]):
                    e, q, r = pairs_of(s, d, p, t)
                    here = (d * sizes[1] + p) * sizes[2] + t
                    pairs.append((here, (e * sizes[1] + q) * sizes[2] + r))
        out.append(lax.ppermute(parts[s], ("dp", "pipe", "tensor"), pairs))
    return out


def over_dp(s, d, p, t):
    return d ^ s, p, t


def over_tensor(s, d, p, t):
    return d, p, t ^ s


def over_dp_on(pipe):
    return lambda s, d, p, t: over_dp(s, d, p, t) if p == pipe else over_tensor(s, d, p, t)


def tied(first, *others):
    return lax.optimization_barrier((first, *others))


def early_pairs(s, d, p, t):
    if p == 1:
        return d ^ s, p, t
    return (d, p, t ^ 1) if s == 1 else (d ^ 1, p, t) if s == 2 else (d, p, t ^ 2)


def handing(packed, n):
    rows = packed.shape[0] - (packed.shape[0] - KERNEL) // 3
    return [packed, packed] + [packed[:rows]] * (n - 2)


def late_pairs(s, d, p, t):
    if p == 0:
        return d ^ s, p, t
    return (d, p, t ^ 1) if s != 2 else (d, p, t ^ 2)


def folded(parts):
    parts = list(parts)
    while len(parts) > 1:
        parts = [parts[i] + parts[i + 1] for i in range(0, len(parts), 2)]
    return parts[0]


def strips(channels):
    return [slice(low, min(low + LANES, channels)) for low in range(0, channels, LANES)]


def valid_rows(count, frames, lanes):
    rows = lax.broadcasted_iota(jnp.int32, (frames, lanes.stop - lanes.start), 0)
    return (rows < count).astype(F32)


def windows(padded, frames, lanes, offsets):
    for low in range(8):
        mine = [k for k in offsets if k % 8 == low]
        whole = padded[low : max(mine) + frames, lanes]
        for k in mine:
            yield k, whole[k - low : k - low + frames]


def cleared(padded, frames):
    padded[:LEFT, :] = jnp.zeros((LEFT, padded.shape[1]), F32)
    padded[LEFT + frames :, :] = jnp.zeros((padded.shape[0] - LEFT - frames, padded.shape[1]), F32)


def below(rows, block, size):
    return slice(rows.start + block * size, rows.stop + block * size)


def coded(sums, lines):
    value = sums[:lines, :]
    head = value.astype(BF16).astype(F32)
    middle = (value - head).astype(BF16).astype(F32)
    rest = value - head - middle
    blank = jnp.zeros((CODE - 3 * lines, value.shape[1]), F32)
    return jnp.concatenate([head, middle, rest, blank]).astype(BF16)


def decoded(ref, lines, lanes):
    value = ref[:CODE, lanes].astype(F32)
    return value[:lines] + value[lines : 2 * lines] + value[2 * lines : 3 * lines]


def column(index, s, channels):
    return pl.ds(pl.multiple_of((index ^ s) * channels, channels), channels)


def share_rows(place, share):
    return pl.ds(pl.multiple_of(place * share, share), share)


def forward_kernel(place, counts, projected, taps, inputs, kept, payload, padded, sums):
    utterances = counts.shape[0]
    size = projected.shape[1]
    frames, channels = size // utterances, projected.shape[2]
    share = payload.shape[1] - CODE
    cleared(padded, frames)
    sums[...] = jnp.zeros_like(sums)
    total = sum(counts[u] for u in range(utterances))
    sums[2:3, :] = jnp.full((1, channels), total, jnp.int32).astype(F32)
    kept[4 * size : 4 * size + KERNEL, :] = taps[...]
    for u in range(utterances):
        rows = slice(u * frames, (u + 1) * frames)
        for lanes in strips(channels):
            valid = valid_rows(counts[u], frames, lanes)
            linear = projected[0, rows, lanes]
            gate = jax.nn.sigmoid(projected[1, rows, lanes])
            value = linear * gate * valid
            kept[below(rows, 0, size), lanes] = linear
            kept[below(rows, 1, size), lanes] = gate
            kept[below(rows, 2, size), lanes] = value
            padded[LEFT : LEFT + frames, lanes] = value
            out = jnp.zeros_like(value)
            for k, window in windows(padded, frames, lanes, range(KERNEL)):
                out += taps[k : k + 1, lanes] * window
            kept[below(rows, 3, size), lanes] = out
            part = out * valid
            sums[0:1, lanes] += jnp.sum(part, axis=0, keepdims=True)
            sums[1:2, lanes] += jnp.sum(part * out, axis=0, keepdims=True)
    code = coded(sums, 3)
    for s in range(payload.shape[0]):
        payload[s, :CODE, :] = code
        payload[s, CODE:, :] = inputs[share_rows(place[1], share), column(place[0], s, channels)]


def scaled_sums(sums, u, lanes, grad_scaled, normed):
    rows = [
        jnp.sum(grad_scaled, axis=0, keepdims=True),
        jnp.sum(grad_scaled * normed, axis=0, keepdims=True),
    ]
    for i, row in enumerate(rows):
        if u == 0:
            sums[i : i + 1, lanes] = row
        else:
            sums[i : i + 1, lanes] += row


def filled(payload, small, place, sums, block, source, share):
    channels = payload.shape[2]
    size = block.shape[0]
    code = coded(sums, 2)
    small[:CODE, :] = code
    small[CODE:, :] = source[
        share_rows(place[1], share), column(place[0], payload.shape[0], channels)
    ]
    for s in range(payload.shape[0]):
        payload[s, :CODE, :] = code
        payload[s, CODE : CODE + size, :] = block[...]
        payload[s, CODE + size :, :] = source[
            share_rows(place[1], share), column(place[0], s, channels)
        ]


def block_of(parts, handed, i, size):
    if i + 1 < len(parts):
        return parts[i][CODE : CODE + size, :]
    return handed[handed.shape[0] - size :, :]


def norm_kernel(place, counts, kept, gain, bias, grad_act, cotangent, *refs):
    *moments, normal, activated, shares, payload, small, sums = refs
    moments = moments[::-1]
    utterances = counts.shape[0]
    size, channels = grad_act.shape
    frames = size // utterances
    share = size // len(moments)
    sums[...] = jnp.zeros_like(sums)
    for s, part in enumerate(moments):
        shares[s * share : (s + 1) * share, :] = part[CODE:, :]
    for lanes in strips(channels):
        moment = folded([decoded(part, 3, lanes) for part in moments])
        total = moment[2:3]
        center = moment[0:1] / total
        inv_std = lax.rsqrt(moment[1:2] / total - center * center + EPSILON)
        normal[3 * size : 3 * size + 1, lanes] = gain[:, lanes] * inv_std
        normal[3 * size + 1 : 3 * size + 2, lanes] = total
        for u in range(utterances):
            rows = slice(u * frames, (u + 1) * frames)
            valid = valid_rows(counts[u], frames, lanes)
            norm = (kept[below(rows, 3, size), lanes] - center) * inv_std
            scaled = gain[:, lanes] * norm + bias[:, lanes]
            squash = jax.nn.sigmoid(scaled)
            steep = valid * squash * (1.0 + scaled * (1.0 - squash))
            grad = grad_act[rows, lanes] * steep
            normal[below(rows, 0, size), lanes] = norm
            normal[below(rows, 1, size), lanes] = steep
            normal[below(rows, 2, size), lanes] = grad
            activated[rows, lanes] = (scaled * squash * valid).astype(BF16)
            scaled_sums(sums, u, lanes, grad, norm)

    @pl.when(place[2] == 1)
    def _():
        filled(payload, small, place, sums, activated, cotangent, share)

    @pl.when(place[2] == 0)
    def _():
        filled(payload, small, place, sums, shares, cotangent, share)


def upstream_kernel(
    parts, place, counts, cotangent, weight, normal, activated, shares, *refs
):
    arrived, (upstream, grad_scaled, payload, small, sums) = refs[:parts], refs[parts:]
    utterances = counts.shape[0]
    size, channels = grad_scaled.shape
    frames = size // utterances
    share = size // parts
    own = cotangent[...]
    total = own.astype(F32) + folded([part[...].astype(F32) for part in arrived])
    whole = jnp.where(place[2] == 1, own, total.astype(BF16))
    upstream[...] = whole
    grad_act = jnp.dot(whole, weight[...], preferred_element_type=F32)
    sums[...] = jnp.zeros_like(sums)
    for u in range(utterances):
        rows = slice(u * frames, (u + 1) * frames)
        for lanes in strips(channels):
            grad = grad_act[rows, lanes] * normal[below(rows, 1, size), lanes]
            grad_scaled[rows, lanes] = grad
            scaled_sums(sums, u, lanes, grad, normal[below(rows, 0, size), lanes])

    @pl.when(place[2] == 1)
    def _():
        filled(payload, small, place, sums, shares, upstream, share)

    @pl.when(place[2] == 0)
    def _():
        filled(payload, small, place, sums, activated, upstream, share)


def gate_kernel(parts, only_later, place, counts, grad_scaled, kept, normal, tap_table, *refs):
    sums, (grad_taps, *earlier, packed, totals_out, padded) = refs[:parts][::-1], refs[parts:]
    utterances = counts.shape[0]
    channels = packed.shape[1]
    size = (packed.shape[0] - KERNEL) // 3
    frames = size // utterances
    base = 2 * size if only_later else 0
    packed[2 * size + KERNEL :, :] = sums[-2][CODE : CODE + size, :]

    def run():
        cleared(padded, frames)
        total = folded([decoded(part, 2, slice(None)) for part in sums])
        for ref in earlier:
            total = jnp.where(place[2] == 1, ref[...], total)
        totals_out[...] = total
        for lanes in strips(channels):
            factor = normal[3 * size : 3 * size + 1, lanes]
            frame_total = normal[3 * size + 1 : 3 * size + 2, lanes]
            bias_part = totals_out[0:1, lanes] / frame_total
            gain_part = totals_out[1:2, lanes] / frame_total
            packed[2 * size : 2 * size + KERNEL, lanes] = (
                factor
                * (
                    grad_taps[:, lanes]
                    - bias_part * tap_table[KERNEL : 2 * KERNEL, lanes]
                    - gain_part * tap_table[:KERNEL, lanes]
                )
            ).astype(BF16)
            for u in range(utterances):
                rows = slice(u * frames, (u + 1) * frames)
                valid = valid_rows(counts[u], frames, lanes)
                grad = grad_scaled[base + rows.start : base + rows.stop, lanes]
                norm = normal[below(rows, 0, size), lanes]
                padded[LEFT : LEFT + frames, lanes] = (
                    factor * (grad - bias_part - norm * gain_part) * valid
                )
                out = jnp.zeros_like(valid)
                for k, window in windows(padded, frames, lanes, range(1, KERNEL + 1)):
                    tap = 4 * size + KERNEL - k
                    out += kept[tap : tap + 1, lanes] * window
                gate = kept[below(rows, 1, size), lanes]
                first = out * valid * gate
                second = first * kept[below(rows, 0, size), lanes] * (1.0 - gate)
                packed[rows, lanes] = first.astype(BF16)
                packed[below(rows, 1, size), lanes] = second.astype(BF16)

    if only_later:
        pl.when(place[2] == 1)(run)
    else:
        run()


def halves_product(packed, planes, size):
    return sum(
        lax.dot_general(
            packed[h * size : (h + 1) * size, :],
            planes[h],
            (((1,), (1,)), ((), ())),
            preferred_element_type=F32,
        )
        for h in range(2)
    )


def first_partial_kernel(place, packed, planes, partial):
    @pl.when(place[2] == 1)
    def _():
        partial[...] = halves_product(packed, planes, partial.shape[0]).astype(BF16)


def last_partial_kernel(parts, place, packed, planes, *refs):
    early, late, (payload, partial) = refs[:parts], refs[parts : 2 * parts], refs[2 * parts :]
    size = partial.shape[0]
    channels = payload.shape[2]
    share = size // parts
    partial[...] = halves_product(packed, planes, size).astype(BF16)
    for s in range(payload.shape[0]):
        payload[s, :size, :] = partial[:, column(place[1], s, channels)]
        for i in range(parts):
            rows = slice(early[i].shape[0] - share, early[i].shape[0])
            value = jnp.where(place[2] == 1, early[i][rows, :], late[i][rows, :])
            payload[s, size + i * share : size + (i + 1) * share, :] = value


def out_kernel(parts, place, upstream, *refs):
    moved, early, late = (refs[i * parts : (i + 1) * parts] for i in range(3))
    moved = moved[::-1]
    early_handed, late_handed, input_grad, out_grad, whole = refs[3 * parts :]
    size, channels = input_grad.shape
    share = size // parts
    total = folded([part[:size, :].astype(F32) for part in moved])
    own = upstream[:, column(place[1], 0, channels)]
    input_grad[...] = (own.astype(F32) + total).astype(BF16)
    for j, part in enumerate(moved):
        for i in range(parts):
            rows = slice(size + i * share, size + (i + 1) * share)
            whole[i, share_rows(place[1] ^ j, share), :] = part[rows, :]
    out_grad[...] = sum(
        lax.dot_general(
            whole[i],
            jnp.where(
                place[2] == 1,
                block_of(early, early_handed, i, size),
                block_of(late, late_handed, i, size),
            ),
            (((0,), (0,)), ((), ())),
            preferred_element_type=F32,
        )
        for i in range(parts)
    )


def inputs_kernel(parts, place, *refs):
    early, late, refs = refs[:parts], refs[parts : 2 * parts], refs[2 * parts :]
    early_handed, late_handed, turned, whole = refs
    size = whole.shape[1]
    share = size // parts
    for j in range(parts):
        value = jnp.where(
            place[2] == 1,
            block_of(late, late_handed, j, size),
            block_of(early, early_handed, j, size),
        )
        for i in range(parts):
            whole[i, share_rows(place[1] ^ j, share), :] = value[i * share : (i + 1) * share]
    for i in range(parts):
        turned[:, i * size : (i + 1) * size] = whole[i].astype(F32).T.astype(BF16)


def glu_kernel(parts, place, *refs):
    early, late, refs = refs[:parts], refs[parts : 2 * parts], refs[2 * parts :]
    inputs, glu_grad, kernel_grad = refs
    early, late = early[::-1], late[::-1]
    size = inputs.shape[1] // parts
    is_later = place[2] == 1
    tail = slice(2 * size, 2 * size + KERNEL)
    for h in range(2):
        rows = slice(h * size, (h + 1) * size)
        both = [jnp.where(is_later, b[rows, :], c[rows, :]) for b, c in zip(early, late)]
        glu_grad[:, h, :] = jnp.dot(
            inputs[...], jnp.concatenate(both), preferred_element_type=F32
        )
    kernel_grad[...] = folded(
        [
            jnp.where(is_later, b[tail, :], c[tail, :]).astype(F32)
            for b, c in zip(early, late)
        ]
    )


def last_kernel(parts, place, *refs):
    first, refs = refs[: 2 * parts + 1], refs[2 * parts + 1 :]
    second, (glu_grad, kernel_grad, *outs) = refs[: 3 * parts + 1], refs[3 * parts + 1 :]
    glu_kernel(parts, place, *first, glu_grad, kernel_grad)
    out_kernel(parts, place, *second, first[parts - 2], first[2 * parts - 2], *outs)


def tap_kernel(base, with_ones, counts, kept, signal, out, padded):
    utterances = counts.shape[0]
    frames, channels = padded.shape[0] - KERNEL, out.shape[1]
    size = utterances * frames
    cleared(padded, frames)
    for lanes in strips(channels):
        for u in range(utterances):
            rows = slice(u * frames, (u + 1) * frames)
            valid = valid_rows(counts[u], frames, lanes)
            padded[LEFT : LEFT + frames, lanes] = kept[below(rows, 2, size), lanes]
            factors = [signal[base + rows.start : base + rows.stop, lanes] * valid]
            factors += [valid] if with_ones else []
            for k, window in windows(padded, frames, lanes, range(KERNEL)):
                for i, factor in enumerate(factors):
                    row = jnp.sum(factor * window, axis=0, keepdims=True)
                    at = slice(i * KERNEL + k, i * KERNEL + k + 1)
                    if u == 0:
                        out[at, lanes] = row
                    else:
                        out[at, lanes] += row


def call(kernel, outs, operands, scratch=(), smem=0, flops=0, place=None):
    if place is not None:
        inner = kernel
        operands, smem = [*place, *operands], smem + len(place)

        def kernel(d, t, p, *refs):
            inner((d[0], t[0], p[0]), *refs)

    moved = sum(x.size * x.dtype.itemsize for x in operands)
    moved += sum(x.size * x.dtype.itemsize for x in outs)
    return pl.pallas_call(
        kernel,
        out_shape=outs,
        in_specs=[SMEM] * smem + [VMEM] * (len(operands) - smem),
        out_specs=[VMEM] * len(outs),
        scratch_shapes=list(scratch),
        compiler_params=pltpu.CompilerParams(vmem_limit_bytes=VMEM_BYTES),
        cost_estimate=pl.CostEstimate(flops=flops, bytes_accessed=moved, transcendentals=0),
    )(*operands)


def paired_shards(
    saved_inputs, cotangent, frame_counts, glu_weight, conv_kernel, norm_gain, norm_bias, out_weight
):
    inputs = saved_inputs[0]
    utterances, frames, width = inputs.shape
    channels = out_weight.shape[-1]
    rows = utterances * frames
    n = lax.axis_size("dp")
    share = rows // n
    place = [lax.axis_index(axis).astype(jnp.int32).reshape(1) for axis in ("dp", "tensor", "pipe")]
    weight = glu_weight[0]
    taps = conv_kernel[0]
    back_weight = out_weight[0]
    inputs_flat = inputs.reshape(rows, width)
    cotangent_flat = cotangent.reshape(rows, width)
    shaped = jax.ShapeDtypeStruct
    taps_shape = shaped((KERNEL, channels), F32)
    block_shape = shaped((rows, channels), BF16)
    padded = pltpu.VMEM((frames + KERNEL, channels), F32)
    table = pltpu.VMEM((8, channels), F32)
    conv_work = 2 * KERNEL * rows * channels

    def product(a, b, dims):
        return lax.dot_general(a, b, (dims, ((), ())), preferred_element_type=F32)

    projected = product(inputs_flat, weight, ((1,), (0,))).transpose(1, 0, 2)
    kept, payload = call(
        forward_kernel,
        [shaped((4 * rows + KERNEL, channels), F32), shaped((n, CODE + share, channels), BF16)],
        [frame_counts, projected, taps, inputs_flat],
        [padded, table],
        smem=1,
        place=place,
        flops=conv_work,
    )
    grad_act = product(cotangent_flat, back_weight, ((1,), (0,)))
    planes = weight.transpose(1, 0, 2)
    moments = swapped(payload, over_dp)
    normal, activated, shares, payload, small = call(
        norm_kernel,
        [
            shaped((3 * rows + 8, channels), F32),
            block_shape,
            block_shape,
            shaped((n - 1, CODE + rows + share, channels), BF16),
            shaped((CODE + share, channels), BF16),
        ],
        [frame_counts, kept, norm_gain, norm_bias, grad_act, cotangent_flat, *moments[::-1]],
        [table],
        smem=1,
        place=place,
    )

    def tap_sums(signal, base, with_ones):
        (out,) = call(
            functools.partial(tap_kernel, base, with_ones),
            [shaped((2 * KERNEL, channels), F32) if with_ones else taps_shape],
            [frame_counts, kept, signal],
            [padded],
            smem=1,
            flops=conv_work,
        )
        return out

    tap_table = tap_sums(normal, 0, True)

    def backward(pipe, grad_scaled, payload, earlier, others):
        parts = swapped(payload, over_dp_on(pipe))
        grad_taps = tap_sums(grad_scaled, 2 * rows if pipe == 1 else 0, False)
        grad_taps, *others = tied(grad_taps, *others)
        packed, total = call(
            functools.partial(gate_kernel, n, pipe == 1),
            [shaped((3 * rows + KERNEL, channels), BF16), shaped((2, channels), F32)],
            [frame_counts, grad_scaled, kept, normal, tap_table, *parts[::-1]]
            + [grad_taps, *earlier],
            [padded],
            smem=1,
            place=place,
            flops=conv_work,
        )
        return packed, total, parts, others

    early, total, early_parts, _ = backward(1, normal, [*payload, small], [], [])
    (partial,) = call(
        first_partial_kernel,
        [shaped((rows, width), BF16)],
        [early, planes],
        flops=4 * rows * width * channels,
        place=place,
    )
    arrived = [
        lax.ppermute(
            partial,
            ("pipe", "tensor"),
            [(n + i, (i + s) % n) for i in range(n)] + [(i, n + i) for i in range(n)],
        )
        for s in range(n)
    ]
    all_early = swapped(handing(early, n), early_pairs)
    upstream, grad_scaled, payload, small = call(
        functools.partial(upstream_kernel, n),
        [
            shaped((rows, width), BF16),
            shaped((rows, channels), F32),
            shaped((n - 1, CODE + rows + share, channels), BF16),
            shaped((CODE + share, channels), BF16),
        ],
        [frame_counts, cotangent_flat, back_weight, normal, activated, shares, *arrived[::-1]],
        [table],
        smem=1,
        place=place,
        flops=2 * rows * width * channels,
    )
    late, total, late_parts, all_early = backward(
        0, grad_scaled, [*payload, small], [total], all_early
    )
    all_late = swapped(handing(late, n), late_pairs)
    (payload,) = call(
        functools.partial(last_partial_kernel, n),
        [shaped((n, 2 * rows, channels), BF16)],
        [late, planes, *early_parts, *late_parts],
        [pltpu.VMEM((rows, width), BF16)],
        flops=4 * rows * width * channels,
        place=place,
    )
    moved = swapped(payload, over_tensor)
    (all_inputs,) = call(
        functools.partial(inputs_kernel, n),
        [shaped((channels, n * rows), BF16)],
        [*early_parts, *late_parts, all_early[1], all_late[1]],
        [pltpu.VMEM((n, rows, channels), BF16)],
        place=place,
    )
    glu_grad, kernel_grad, input_grad, out_grad = call(
        functools.partial(last_kernel, n),
        [
            shaped((channels, 2, channels), F32),
            taps_shape,
            block_shape,
            shaped((channels, channels), F32),
        ],
        [
            *all_early[::-1],
            *all_late[::-1],
            all_inputs,
            upstream,
            *moved[::-1],
            *early_parts,
            *late_parts,
        ],
        [pltpu.VMEM((n, rows, channels), BF16)],
        flops=6 * rows * width * channels,
        place=place,
    )
    return (
        input_grad.reshape(1, utterances, frames, channels),
        glu_grad[None],
        out_grad[None],
        kernel_grad[None],
        total[1:2],
        total[0:1],
    )


def solution(mesh):
    placed = (
        P("pipe", "dp", None, None),
        P("dp", None, None),
        P("dp"),
        P("pipe", None, None, "tensor"),
        P("pipe", None, "tensor"),
        P("pipe", "tensor"),
        P("pipe", "tensor"),
        P("pipe", None, "tensor"),
    )
    n = mesh.shape["dp"]
    paired = n == mesh.shape["tensor"] == 4 and mesh.shape["pipe"] == 2
    return jax.shard_map(
        paired_shards if paired else general_shards,
        mesh=mesh,
        in_specs=placed,
        out_specs=(
            P("pipe", "dp", None, "tensor"),
            P("pipe", "dp", None, "tensor"),
            P("pipe", "dp", "tensor"),
            P("pipe", None, "tensor"),
            P("pipe", "tensor"),
            P("pipe", "tensor"),
        ),
        check_vma=False,
    )
```
